32 devices in a mesh: group: 1, expert: 16 (over z, y, x), tensor: 2 (over core).
Axes of the slice: x: 2, y: 2, z: 4, core: 2. Of those that a mesh axis runs over, the one named last changes fastest.
Arguments:
- resid: bfloat16 [3072, 4096], P(('group', 'expert'), 'tensor'), as said below
- context: bfloat16 [3072, 4096], P(('group', 'expert')), may hold values from -6 to 6
- out_weight: bfloat16 [4096, 4096], P('expert', 'tensor'), may hold values from -0.09375 to 0.09375
- norm_gain: float32 [4096], replicated, may hold values from 0.1 to 1.9
- gate_up: bfloat16 [16, 2, 4096, 768], P('expert', None, None, 'tensor'), may hold values from -0.09375 to 0.09375
- down_weight: bfloat16 [16, 768, 4096], P('expert', None, 'tensor'), may hold values from -0.21875 to 0.21875
- expert_ids: int32 [3072, 8], P(('group', 'expert')), may hold values from 0 to 127, as said below
- slots: int32 [3072, 8], P(('group', 'expert')), may hold values from -1 to 23, as said below
- token_order: int32 [256, 24], P(('group', 'expert')), may hold values from -1 to 191, as said below
- combine: float32 [3072, 8], P(('group', 'expert')), may hold values from 0.1 to 0.6
Outputs:
- mixed: bfloat16 [3072, 4096], P(('group', 'expert'), 'tensor')
The draws below stay inside these ranges and needn't reach their ends.
Inputs may be any that keep to these rules, and one draw needn't show every extreme that they name: `expert_ids`: each row names 8 different experts of the model's 128; only those under 16 are in flight. `slots`: for a choice of an expert in flight, its place among the rows that the token's index of expert sends to that expert, counted in order of token and then choice; -1 where the expert is not in flight or 24 rows came before it. `token_order`: row s * 16 + m holds, for each slot c, the token (numbered within index s) whose choice has expert m and slot c, or -1 where no choice has it; it agrees with expert_ids and slots. `resid`: rows of a few tokens to several features of order one; their scales differ from token to token and from feature to feature.
All inputs are finite; a program needn't handle non-finite values.
Results may differ from the reference program's by a relative error of at most 0.0043.
Values may be sent and summed in bfloat16 or wider, within the bound.
A program may use at most 128 MiB of HBM per device.

```python
import jax
import jax.numpy as jnp
from jax import lax

D = 4096
HEADS = 32
HEAD_DIM = 128
FFE = 768
ALL_EXPERTS = 128
TOP = 8
TOK_E = 192
CAP = 24
EXPERTS = 16
TOKENS = 3072
N_EXPERT = 16


def route_tables(key):
    first_key, second_key, third_key = jax.random.split(key, 3)
    blocks = TOKENS // TOK_E
    level = jax.random.randint(first_key, (ALL_EXPERTS,), 0, 3)
    hottest = jax.random.randint(second_key, (), 0, EXPERTS)
    coldest = (hottest + 1) % EXPERTS
    numbers = jnp.arange(ALL_EXPERTS, dtype=jnp.int32)
    level = jnp.where(numbers == ALL_EXPERTS - 1, 3, level)
    level = jnp.where(numbers == coldest, 0, level)
    level = jnp.where(numbers == hottest, 4, level)
    noise = jax.random.randint(third_key, (TOKENS, ALL_EXPERTS), 0, 1024)
    token_numbers = jnp.arange(TOKENS, dtype=jnp.int32)
    block_of = token_numbers // TOK_E
    local_of = token_numbers % TOK_E
    boost = jnp.where((local_of[:, None] == TOK_E - 1) & (numbers[None, :] == coldest), 6000, 0)
    score = (noise + 800 * level[None, :] + boost) * ALL_EXPERTS + numbers[None, :]
    unused, expert_ids = lax.top_k(score, TOP)
    expert_ids = expert_ids.astype(jnp.int32)
    onehot = (expert_ids[:, :, None] == jnp.arange(EXPERTS, dtype=jnp.int32)[None, None, :]).astype(jnp.int32)
    onehot = onehot.reshape(blocks, TOK_E * TOP, EXPERTS)
    before = jnp.cumsum(onehot, axis=1) - onehot
    place = jnp.sum(before * onehot, axis=2).reshape(TOKENS, TOP)
    usable = (expert_ids < EXPERTS) & (place < CAP)
    slots = jnp.where(usable, place, -1).astype(jnp.int32)
    limit = blocks * EXPERTS * CAP
    target = jnp.where(usable, (block_of[:, None] * EXPERTS + expert_ids) * CAP + slots, limit)
    filler = jnp.broadcast_to(local_of[:, None], (TOKENS, TOP))
    order_flat = jnp.full((limit,), -1, jnp.int32).at[target.reshape(-1)].set(filler.reshape(-1), mode='drop')
    return (expert_ids, slots, order_flat.reshape(blocks * EXPERTS, CAP))


def draw_expert_ids(key, part):
    return route_tables(key)[0]


def draw_slots(key, part):
    return route_tables(key)[1]


def draw_token_order(key, part):
    return route_tables(key)[2]


def draw_resid(key, part):
    key = jax.random.fold_in(key, 11)
    first_key, second_key, third_key = jax.random.split(key, 3)
    ramp = jnp.arange(D, dtype=jnp.float32)[None, :] / D
    row_scale = jnp.exp(jax.random.uniform(second_key, (TOKENS, 1), jnp.float32, jnp.log(0.3), jnp.log(3.0)))
    column_scale = jnp.exp(jax.random.uniform(third_key, (1, D), jnp.float32, jnp.log(0.5), jnp.log(2.0)) + jnp.log(3.0) * ramp) / 1.7
    values = jax.random.normal(first_key, (TOKENS, D), jnp.float32)
    return (values * row_scale * column_scale).astype(jnp.bfloat16)


def level_of(stream_key, dims, cuts, smallest, top_value):
    def one(position, shards_of):
        heights = jax.random.uniform(jax.random.fold_in(jax.random.fold_in(stream_key, 6), position), (shards_of,), jnp.float32, smallest / len(cuts), top_value / len(cuts))
        return jnp.repeat(jnp.exp(heights), dims[position] // shards_of).reshape((-1,) + (1,) * (len(dims) - position - 1))

    gain = one(*cuts[0])
    for cut in cuts[1:]:
        gain = gain * one(*cut)
    return gain


def normal_values(key, dims, deviation, most, pieces=(), kind=jnp.bfloat16):
    values = deviation * jax.random.normal(key, dims, jnp.float32)
    if pieces:
        values = values * level_of(key, dims, pieces, -0.22, 0.18)
    return jnp.clip(values, -most, most).astype(kind)


def setup_inputs(seed: int = 0, part: int = 0) -> dict:
    streams_of = jax.random.split(jax.random.key(seed), 11)
    own_keys = jax.random.split(jax.random.fold_in(streams_of[10], part), 11)
    return {
        "resid": draw_resid(jax.random.fold_in(jax.random.fold_in(streams_of[10], part), 71), part),
        "context": normal_values(own_keys[1], (TOKENS, HEADS * HEAD_DIM), 1.0, 6.0, ((0, 16),)),
        "out_weight": normal_values(streams_of[2], (HEADS * HEAD_DIM, D), (HEADS * HEAD_DIM) ** -0.5, 0.09375, ((0, 16), (1, 2))),
        "norm_gain": jnp.clip(1.0 + 0.18 * jax.random.normal(streams_of[3], (D,), jnp.float32), 0.1, 1.9),
        "gate_up": normal_values(streams_of[4], (EXPERTS, 2, D, FFE), D ** -0.5, 0.09375, ((0, 16), (3, 2))),
        "down_weight": normal_values(streams_of[5], (EXPERTS, FFE, D), FFE ** -0.5, 0.21875, ((0, 16), (2, 2))),
        "expert_ids": draw_expert_ids(jax.random.fold_in(jax.random.fold_in(streams_of[10], part), 71), part),
        "slots": draw_slots(jax.random.fold_in(jax.random.fold_in(streams_of[10], part), 71), part),
        "token_order": draw_token_order(jax.random.fold_in(jax.random.fold_in(streams_of[10], part), 71), part),
        "combine": jnp.clip(0.1 + 0.5 * jax.random.uniform(own_keys[9], (TOKENS, TOP), jnp.float32) ** level_of(own_keys[9], (TOKENS, TOP), ((0, 16),), -0.2, 0.2), 0.1, 0.6),
    }


epsilon = 1e-06

def reference(resid, context, out_weight, norm_gain, gate_up, down_weight, expert_ids, slots, token_order, combine):
    attention = jnp.dot(context, out_weight, preferred_element_type=jnp.float32)
    hidden_state = (resid.astype(jnp.float32) + attention).astype(jnp.bfloat16)
    state_float = hidden_state.astype(jnp.float32)
    row_scale = lax.rsqrt(lax.optimization_barrier(jnp.mean(state_float * state_float, axis=1, keepdims=True)) + epsilon)
    normed = (state_float * row_scale * norm_gain).astype(jnp.bfloat16)
    order_blocks = token_order.reshape(N_EXPERT, EXPERTS, CAP)
    base_rows = (jnp.arange(N_EXPERT, dtype=jnp.int32) * TOK_E)[:, None, None]
    global_rows = jnp.where(order_blocks >= 0, order_blocks + base_rows, 0).astype(jnp.int32)
    occupied = order_blocks >= 0

    def run_expert(index):
        pick_rows = lax.dynamic_index_in_dim(global_rows, index, 1, keepdims=False).reshape(-1)
        keep_rows = lax.dynamic_index_in_dim(occupied, index, 1, keepdims=False).reshape(-1)
        inputs = jnp.where(keep_rows[:, None], normed[pick_rows], jnp.zeros((), jnp.bfloat16))
        weights = lax.dynamic_index_in_dim(gate_up, index, 0, keepdims=False)
        gate_part = jnp.dot(inputs, weights[0], preferred_element_type=jnp.float32)
        up_part = jnp.dot(inputs, weights[1], preferred_element_type=jnp.float32)
        active = (jax.nn.silu(gate_part) * up_part).astype(jnp.bfloat16)
        down_part = lax.dynamic_index_in_dim(down_weight, index, 0, keepdims=False)
        return jnp.dot(active, down_part, preferred_element_type=jnp.float32).astype(jnp.bfloat16)
    outputs = lax.map(run_expert, jnp.arange(EXPERTS, dtype=jnp.int32))
    back_table = outputs.reshape(-1, D)
    source = jnp.arange(TOKENS, dtype=jnp.int32) // TOK_E
    live_slot = slots >= 0
    flat_index = jnp.where(live_slot, (expert_ids * N_EXPERT + source[:, None]) * CAP + slots, 0).astype(jnp.int32)
    mixed_sum = jnp.zeros((TOKENS, D), jnp.float32)
    for column in range(TOP):
        got_rows = back_table[flat_index[:, column]].astype(jnp.float32)
        weight = jnp.where(live_slot[:, column], combine[:, column], jnp.zeros((), jnp.float32))
        mixed_sum = mixed_sum + weight[:, None] * got_rows
    return (state_float + mixed_sum).astype(jnp.bfloat16)
```

```python
import jax
import jax.numpy as jnp
from jax import lax
from jax.sharding import PartitionSpec as P

epsilon = 1e-06


def per_device(
    resid,
    context,
    out_weight,
    norm_gain,
    gate_up,
    down_weight,
    expert_ids,
    slots,
    token_order,
    combine,
):
    tok_rows, half_width = resid.shape
    members = lax.axis_size("expert")
    near = 4
    far = members // near
    planes = [[p * near + i for i in range(near)] for p in range(far)]
    lines = [[p * near + i for p in range(far)] for i in range(near)]
    pair_side = lax.axis_index("tensor")
    k_rows = out_weight.shape[0]
    plane_weight = lax.all_gather(out_weight, "expert", axis=0, tiled=True, axis_index_groups=planes)
    context_parts = context.reshape(tok_rows, far, near * k_rows).transpose(1, 0, 2)
    line_context = lax.all_to_all(
        context_parts, "expert", split_axis=0, concat_axis=0, tiled=True, axis_index_groups=lines
    )
    partial = jnp.dot(
        line_context.reshape(far * tok_rows, near * k_rows), plane_weight, preferred_element_type=jnp.float32
    ).astype(jnp.bfloat16)
    parts = lax.all_to_all(
        partial.reshape(far, tok_rows, half_width),
        "expert",
        split_axis=0,
        concat_axis=0,
        tiled=True,
        axis_index_groups=lines,
    )
    attention = jnp.sum(parts.astype(jnp.float32), axis=0)
    hidden_state = (resid.astype(jnp.float32) + attention).astype(jnp.bfloat16)
    state_float = hidden_state.astype(jnp.float32)
    width = norm_gain.shape[0]
    squares = lax.psum(jnp.sum(state_float * state_float, axis=1, keepdims=True), "tensor")
    row_scale = lax.rsqrt(squares / width + epsilon)
    gain = lax.dynamic_slice_in_dim(norm_gain, pair_side * half_width, half_width)
    normed = (state_float * row_scale * gain).astype(jnp.bfloat16)
    capacity = token_order.shape[1]
    tokens = jnp.arange(tok_rows, dtype=jnp.int32)
    pick = (token_order.reshape(-1, 1) == tokens[None, :]).astype(jnp.bfloat16)
    packed = jnp.dot(pick, normed, preferred_element_type=jnp.float32).astype(jnp.bfloat16)
    packed = packed.reshape(members, capacity, half_width)
    features = lax.all_to_all(packed, "expert", split_axis=0, concat_axis=0, tiled=True)
    flat_rows = features.reshape(members * capacity, half_width)
    flat_rows = lax.all_gather(flat_rows, "tensor", axis=1, tiled=True)
    gate_part = jnp.dot(flat_rows, gate_up[0, 0], preferred_element_type=jnp.float32)
    up_part = jnp.dot(flat_rows, gate_up[0, 1], preferred_element_type=jnp.float32)
    active = (jax.nn.silu(gate_part) * up_part).astype(jnp.bfloat16)
    active = lax.all_gather(active, "tensor", axis=1, tiled=True)
    product = jnp.dot(active, down_weight[0], preferred_element_type=jnp.float32)
    product = product.astype(jnp.bfloat16).reshape(members, capacity, half_width)
    returned = lax.all_to_all(product, "expert", split_axis=0, concat_axis=0, tiled=True)
    flat_index = jnp.where(slots >= 0, expert_ids * capacity + slots, -1)
    places = jnp.arange(members * capacity, dtype=jnp.int32)
    weights = jnp.zeros((tok_rows, members * capacity), jnp.float32)
    for column in range(expert_ids.shape[1]):
        weights = weights + jnp.where(flat_index[:, column, None] == places[None, :], combine[:, column, None], 0.0)
    high = lax.reduce_precision(weights, 8, 7)
    middle = lax.reduce_precision(weights - high, 8, 7)
    low = weights - high - middle
    table = returned.reshape(-1, half_width)
    three = jnp.concatenate([high, middle, low], axis=0).astype(jnp.bfloat16)
    sums = jnp.dot(three, table, preferred_element_type=jnp.float32)
    mixed_sum = jnp.sum(sums.reshape(3, tok_rows, half_width), axis=0)
    return (state_float + mixed_sum).astype(jnp.bfloat16)


def solution(mesh):
    placed = (
        P(("group", "expert"), "tensor"),
        P(("group", "expert"), None),
        P("expert", "tensor"),
        P(),
        P("expert", None, None, "tensor"),
        P("expert", None, "tensor"),
        P(("group", "expert"), None),
        P(("group", "expert"), None),
        P(("group", "expert"), None),
        P(("group", "expert"), None),
    )
    return jax.shard_map(
        per_device,
        mesh=mesh,
        in_specs=placed,
        out_specs=P(("group", "expert"), "tensor"),
        check_vma=False,
    )
```

```python
import functools

import jax
import jax.numpy as jnp
from jax import lax
from jax.experimental import pallas as pl
from jax.experimental.pallas import tpu as pltpu
from jax.sharding import PartitionSpec as P

epsilon = 1e-06
near = 4
chunks = 4


def attention_kernel(
    members,
    resid,
    context,
    weight,
    hidden,
    plane_weight,
    line_context,
    sums,
    outgoing,
    from_left,
    from_right,
    own_sem,
    weight_send,
    weight_recv,
    context_send,
    context_recv,
    share_send,
    share_recv,
    chain_send,
    left_recv,
    right_recv,
):
    far = members // near
    me = lax.axis_index("expert")
    side = lax.axis_index("tensor")
    line = lax.div(me, near)
    spot = lax.rem(me, near)
    rows, half = resid.shape
    depth = weight.shape[0]
    span = near * depth
    piece = span // 2
    wide = half // chunks

    def columns(c):
        return pl.ds(pl.multiple_of(c * wide, wide), wide)

    def token_rows(q):
        return pl.ds(pl.multiple_of(q * rows, rows), rows)

    own_columns = pl.ds(pl.multiple_of(side * piece, piece), piece)

    def weight_copy(d, c):
        slot = pl.ds(pl.multiple_of(spot * depth, depth), depth)
        return pltpu.make_async_remote_copy(
            src_ref=weight.at[:, columns(c)],
            dst_ref=plane_weight.at[slot, columns(c)],
            send_sem=weight_send.at[d, c],
            recv_sem=weight_recv.at[d, c],
            device_id={"expert": line * near + lax.bitwise_xor(spot, d)},
            device_id_type=pl.DeviceIdType.MESH,
        )

    def context_copy(d):
        target = lax.rem(line + d, far)
        return pltpu.make_async_remote_copy(
            src_ref=context.at[:, pl.ds(pl.multiple_of(target * span + side * piece, piece), piece)],
            dst_ref=line_context.at[token_rows(line), own_columns],
            send_sem=context_send.at[d],
            recv_sem=context_recv.at[d],
            device_id={"expert": target * near + spot},
            device_id_type=pl.DeviceIdType.MESH,
        )

    def share_copy(d):
        place = line_context.at[token_rows(lax.rem(line - d + far, far)), own_columns]
        return pltpu.make_async_remote_copy(
            src_ref=place,
            dst_ref=place,
            send_sem=share_send.at[d],
            recv_sem=share_recv.at[d],
            device_id={"tensor": 1 - side},
            device_id_type=pl.DeviceIdType.MESH,
        )

    def right_copy(q, c):
        return pltpu.make_async_remote_copy(
            src_ref=outgoing.at[token_rows(q), columns(c)],
            dst_ref=from_left.at[token_rows(q), columns(c)],
            send_sem=chain_send.at[q, c],
            recv_sem=left_recv.at[q, c],
            device_id={"expert": me + near},
            device_id_type=pl.DeviceIdType.MESH,
        )

    def left_copy(q, c):
        return pltpu.make_async_remote_copy(
            src_ref=outgoing.at[token_rows(q), columns(c)],
            dst_ref=from_right.at[token_rows(q), columns(c)],
            send_sem=chain_send.at[q, c],
            recv_sem=right_recv.at[q, c],
            device_id={"expert": me - near},
            device_id_type=pl.DeviceIdType.MESH,
        )

    barrier = pltpu.get_barrier_semaphore()
    for d in range(1, near):
        pl.semaphore_signal(
            barrier,
            inc=1,
            device_id={"expert": line * near + lax.bitwise_xor(spot, d)},
            device_id_type=pl.DeviceIdType.MESH,
        )
    for d in range(1, far):
        pl.semaphore_signal(
            barrier,
            inc=1,
            device_id={"expert": lax.rem(line + d, far) * near + spot},
            device_id_type=pl.DeviceIdType.MESH,
        )
    pl.semaphore_signal(barrier, inc=1, device_id={"tensor": 1 - side}, device_id_type=pl.DeviceIdType.MESH)
    own_weight = pltpu.make_async_copy(
        weight, plane_weight.at[pl.ds(pl.multiple_of(spot * depth, depth), depth), :], own_sem.at[0]
    )
    own_context = pltpu.make_async_copy(
        context.at[:, pl.ds(pl.multiple_of(line * span, span), span)],
        line_context.at[token_rows(line), :],
        own_sem.at[1],
    )
    own_weight.start()
    own_context.start()
    pl.semaphore_wait(barrier, near + far - 1)

    for d in range(1, far):
        context_copy(d).start()
    for c in range(chunks):
        for d in (3, 1, 2):
            weight_copy(d, c).start()
    own_weight.wait()
    own_context.wait()
    for d in range(1, far):
        context_copy(d).wait_recv()
        share_copy(d).start()
    for d in range(1, far):
        share_copy(d).wait_recv()

    def multiply(c):
        for d in range(1, near):
            weight_copy(d, c).wait_recv()

        def block(k, carry):
            q = lax.select(line * 2 < far, far - 1 - k, k)
            sums[token_rows(q), columns(c)] = jnp.dot(
                line_context[token_rows(q), :], plane_weight[:, columns(c)], preferred_element_type=jnp.float32
            )

            @pl.when((line == 0) & (q > 0))
            def _():
                outgoing[token_rows(q), columns(c)] = sums[token_rows(q), columns(c)].astype(jnp.bfloat16)
                right_copy(q, c).start()

            @pl.when((line == far - 1) & (q < far - 1))
            def _():
                outgoing[token_rows(q), columns(c)] = sums[token_rows(q), columns(c)].astype(jnp.bfloat16)
                left_copy(q, c).start()

            return carry

        lax.fori_loop(0, far, block, 0)

    def pass_right(c):
        def block(k, carry):
            q = far - 1 - k
            right_copy(q, c).wait_recv()
            total = sums[token_rows(q), columns(c)] + from_left[token_rows(q), columns(c)].astype(jnp.float32)
            outgoing[token_rows(q), columns(c)] = total.astype(jnp.bfloat16)
            right_copy(q, c).start()
            return carry

        lax.fori_loop(0, lax.select(line > 0, far - 1 - line, 0), block, 0)

    def pass_left(c):
        def block(q, carry):
            left_copy(q, c).wait_recv()
            total = sums[token_rows(q), columns(c)] + from_right[token_rows(q), columns(c)].astype(jnp.float32)
            outgoing[token_rows(q), columns(c)] = total.astype(jnp.bfloat16)
            left_copy(q, c).start()
            return carry

        lax.fori_loop(0, lax.select(line < far - 1, line, 0), block, 0)

    def forward(c):
        @pl.when(line * 2 < far)
        def _():
            pass_right(c)
            pass_left(c)

        @pl.when(line * 2 >= far)
        def _():
            pass_left(c)
            pass_right(c)

    def step(c, carry):
        multiply(c)

        @pl.when(c > 0)
        def _():
            forward(c - 1)

        return carry

    lax.fori_loop(0, chunks, step, 0)
    forward(chunks - 1)

    def finish(c, carry):
        sums[token_rows(line), columns(c)] += resid[:, columns(c)].astype(jnp.float32)

        @pl.when(line > 0)
        def _():
            right_copy(line, c).wait_recv()
            sums[token_rows(line), columns(c)] += from_left[token_rows(line), columns(c)].astype(jnp.float32)

        @pl.when(line < far - 1)
        def _():
            left_copy(line, c).wait_recv()
            sums[token_rows(line), columns(c)] += from_right[token_rows(line), columns(c)].astype(jnp.float32)

        hidden[:, columns(c)] = sums[token_rows(line), columns(c)].astype(jnp.bfloat16)
        return carry

    lax.fori_loop(0, chunks, finish, 0)

    for d in range(1, far):
        context_copy(d).wait_send()
        share_copy(d).wait_send()

    def drain(c, carry):
        for d in range(1, near):
            weight_copy(d, c).wait_send()

        def right_done(q, inner):
            right_copy(q, c).wait_send()
            return inner

        def left_done(q, inner):
            left_copy(q, c).wait_send()
            return inner

        lax.fori_loop(line + 1, far, right_done, 0)
        lax.fori_loop(0, line, left_done, 0)
        return carry

    lax.fori_loop(0, chunks, drain, 0)


def projected(resid, context, out_weight):
    members = lax.axis_size("expert")
    far = members // near
    rows, half = resid.shape
    depth = out_weight.shape[0]
    dma = pltpu.SemaphoreType.DMA
    return pl.pallas_call(
        functools.partial(attention_kernel, members),
        out_shape=jax.ShapeDtypeStruct((rows, half), jnp.bfloat16),
        in_specs=[pl.BlockSpec(memory_space=pltpu.VMEM)] * 3,
        out_specs=pl.BlockSpec(memory_space=pltpu.VMEM),
        scratch_shapes=[
            pltpu.VMEM((near * depth, half), jnp.bfloat16),
            pltpu.VMEM((far * rows, near * depth), jnp.bfloat16),
            pltpu.VMEM((far * rows, half), jnp.float32),
            pltpu.VMEM((far * rows, half), jnp.bfloat16),
            pltpu.VMEM((far * rows, half), jnp.bfloat16),
            pltpu.VMEM((far * rows, half), jnp.bfloat16),
            dma((2,)),
            dma((near, chunks)),
            dma((near, chunks)),
            dma((far,)),
            dma((far,)),
            dma((far,)),
            dma((far,)),
            dma((far, chunks)),
            dma((far, chunks)),
            dma((far, chunks)),
        ],
        compiler_params=pltpu.CompilerParams(
            collective_id=0, has_side_effects=True, vmem_limit_bytes=58 * 2**20
        ),
        name="projection",
    )(resid, context, out_weight)


def per_device(
    resid,
    context,
    out_weight,
    norm_gain,
    gate_up,
    down_weight,
    expert_ids,
    slots,
    token_order,
    combine,
):
    tok_rows, half_width = resid.shape
    members = lax.axis_size("expert")
    pair_side = lax.axis_index("tensor")
    hidden_state = projected(resid, context, out_weight)
    state_float = hidden_state.astype(jnp.float32)
    width = norm_gain.shape[0]
    squares = lax.psum(jnp.sum(state_float * state_float, axis=1, keepdims=True), "tensor")
    row_scale = lax.rsqrt(squares / width + epsilon)
    gain = lax.dynamic_slice_in_dim(norm_gain, pair_side * half_width, half_width)
    normed = (state_float * row_scale * gain).astype(jnp.bfloat16)
    capacity = token_order.shape[1]
    tokens = jnp.arange(tok_rows, dtype=jnp.int32)
    pick = (token_order.reshape(-1, 1) == tokens[None, :]).astype(jnp.bfloat16)
    packed = jnp.dot(pick, normed, preferred_element_type=jnp.float32).astype(jnp.bfloat16)
    packed = packed.reshape(members, capacity, half_width)
    features = lax.all_to_all(packed, "expert", split_axis=0, concat_axis=0, tiled=True)
    flat_rows = features.reshape(members * capacity, half_width)
    flat_rows = lax.all_gather(flat_rows, "tensor", axis=1, tiled=True)
    gate_part = jnp.dot(flat_rows, gate_up[0, 0], preferred_element_type=jnp.float32)
    up_part = jnp.dot(flat_rows, gate_up[0, 1], preferred_element_type=jnp.float32)
    active = (jax.nn.silu(gate_part) * up_part).astype(jnp.bfloat16)
    active = lax.all_gather(active, "tensor", axis=1, tiled=True)
    product = jnp.dot(active, down_weight[0], preferred_element_type=jnp.float32)
    product = product.astype(jnp.bfloat16).reshape(members, capacity, half_width)
    returned = lax.all_to_all(product, "expert", split_axis=0, concat_axis=0, tiled=True)
    flat_index = jnp.where(slots >= 0, expert_ids * capacity + slots, -1)
    places = jnp.arange(members * capacity, dtype=jnp.int32)
    weights = jnp.zeros((tok_rows, members * capacity), jnp.float32)
    for column in range(expert_ids.shape[1]):
        weights = weights + jnp.where(flat_index[:, column, None] == places[None, :], combine[:, column, None], 0.0)
    high = lax.reduce_precision(weights, 8, 7)
    middle = lax.reduce_precision(weights - high, 8, 7)
    low = weights - high - middle
    table = returned.reshape(-1, half_width)
    three = jnp.concatenate([high, middle, low], axis=0).astype(jnp.bfloat16)
    sums = jnp.dot(three, table, preferred_element_type=jnp.float32)
    mixed_sum = jnp.sum(sums.reshape(3, tok_rows, half_width), axis=0)
    return (state_float + mixed_sum).astype(jnp.bfloat16)


def solution(mesh):
    placed = (
        P(("group", "expert"), "tensor"),
        P(("group", "expert"), None),
        P("expert", "tensor"),
        P(),
        P("expert", None, None, "tensor"),
        P("expert", None, "tensor"),
        P(("group", "expert"), None),
        P(("group", "expert"), None),
        P(("group", "expert"), None),
        P(("group", "expert"), None),
    )
    return jax.shard_map(
        per_device,
        mesh=mesh,
        in_specs=placed,
        out_specs=P(("group", "expert"), "tensor"),
        check_vma=False,
    )
```

```python
import functools

import jax
import jax.numpy as jnp
from jax import lax
from jax.experimental import pallas as pl
from jax.experimental.pallas import tpu as pltpu
from jax.sharding import PartitionSpec as P

epsilon = 1e-06
near = 4
chunks = 4


def layer_kernel(
    members,
    resid,
    context,
    weight,
    gain,
    pick,
    gate_up,
    down_weight,
    hidden,
    returned,
    plane_weight,
    line_context,
    sums,
    travel,
    squares,
    stacked,
    packed,
    features,
    gate_up_local,
    down_local,
    active,
    product,
    own_sem,
    weight_send,
    weight_recv,
    context_send,
    context_recv,
    share_send,
    share_recv,
    chain_send,
    left_recv,
    right_recv,
    square_send,
    square_recv,
    row_send,
    row_recv,
    pair_send,
    pair_recv,
    active_send,
    active_recv,
    back_send,
    back_recv,
):
    far = members // near
    me = lax.axis_index("expert")
    side = lax.axis_index("tensor")
    line = lax.div(me, near)
    spot = lax.rem(me, near)
    rows, half = resid.shape
    depth = weight.shape[0]
    span = near * depth
    piece = span // 2
    wide = half // chunks

    def columns(c):
        return pl.ds(pl.multiple_of(c * wide, wide), wide)

    def token_rows(q):
        return pl.ds(pl.multiple_of(q * rows, rows), rows)

    own_columns = pl.ds(pl.multiple_of(side * piece, piece), piece)

    def weight_copy(d, c):
        slot = pl.ds(pl.multiple_of(spot * depth, depth), depth)
        return pltpu.make_async_remote_copy(
            src_ref=weight.at[:, columns(c)],
            dst_ref=plane_weight.at[slot, columns(c)],
            send_sem=weight_send.at[d, c],
            recv_sem=weight_recv.at[d, c],
            device_id={"expert": line * near + lax.bitwise_xor(spot, d)},
            device_id_type=pl.DeviceIdType.MESH,
        )

    def context_copy(d):
        target = lax.rem(line + d, far)
        return pltpu.make_async_remote_copy(
            src_ref=context.at[:, pl.ds(pl.multiple_of(target * span + side * piece, piece), piece)],
            dst_ref=line_context.at[token_rows(line), own_columns],
            send_sem=context_send.at[d],
            recv_sem=context_recv.at[d],
            device_id={"expert": target * near + spot},
            device_id_type=pl.DeviceIdType.MESH,
        )

    def share_copy(d):
        place = line_context.at[token_rows(lax.rem(line - d + far, far)), own_columns]
        return pltpu.make_async_remote_copy(
            src_ref=place,
            dst_ref=place,
            send_sem=share_send.at[d],
            recv_sem=share_recv.at[d],
            device_id={"tensor": 1 - side},
            device_id_type=pl.DeviceIdType.MESH,
        )

    def right_copy(q, c):
        return pltpu.make_async_remote_copy(
            src_ref=travel.at[token_rows(q), columns(c)],
            dst_ref=travel.at[token_rows(q), columns(c)],
            send_sem=chain_send.at[q, c],
            recv_sem=left_recv.at[q, c],
            device_id={"expert": me + near},
            device_id_type=pl.DeviceIdType.MESH,
        )

    def left_copy(q, c):
        return pltpu.make_async_remote_copy(
            src_ref=travel.at[token_rows(q), columns(c)],
            dst_ref=travel.at[token_rows(lax.select(q == line - 1, far, q)), columns(c)],
            send_sem=chain_send.at[q, c],
            recv_sem=right_recv.at[q, c],
            device_id={"expert": me - near},
            device_id_type=pl.DeviceIdType.MESH,
        )

    barrier = pltpu.get_barrier_semaphore()
    def greet(d, carry):
        pl.semaphore_signal(
            barrier,
            inc=1,
            device_id={"expert": lax.rem(me + d, members)},
            device_id_type=pl.DeviceIdType.MESH,
        )
        return carry

    lax.fori_loop(1, members, greet, 0)
    pl.semaphore_signal(barrier, inc=1, device_id={"tensor": 1 - side}, device_id_type=pl.DeviceIdType.MESH)
    own_weight = pltpu.make_async_copy(
        weight, plane_weight.at[pl.ds(pl.multiple_of(spot * depth, depth), depth), :], own_sem.at[0]
    )
    own_context = pltpu.make_async_copy(
        context.at[:, pl.ds(pl.multiple_of(line * span, span), span)],
        line_context.at[token_rows(line), :],
        own_sem.at[1],
    )
    own_weight.start()
    own_context.start()
    pl.semaphore_wait(barrier, members)

    for d in range(1, far):
        context_copy(d).start()
    for c in range(chunks):
        for d in (3, 1, 2):
            weight_copy(d, c).start()
    ffe = gate_up.shape[3]
    loads = [
        pltpu.make_async_copy(gate_up.at[0, 0], gate_up_local.at[:, :ffe], own_sem.at[2]),
        pltpu.make_async_copy(gate_up.at[0, 1], gate_up_local.at[:, ffe:], own_sem.at[3]),
        pltpu.make_async_copy(down_weight.at[0], down_local, own_sem.at[4]),
    ]
    for load in loads:
        load.start()
    own_weight.wait()
    own_context.wait()
    for d in range(1, far):
        context_copy(d).wait_recv()
        share_copy(d).start()
    for d in range(1, far):
        share_copy(d).wait_recv()

    def multiply(c):
        for d in range(1, near):
            weight_copy(d, c).wait_recv()

        def block(k, carry):
            q = lax.select(line * 2 < far, far - 1 - k, k)
            sums[token_rows(q), columns(c)] = jnp.dot(
                line_context[token_rows(q), :], plane_weight[:, columns(c)], preferred_element_type=jnp.float32
            )

            @pl.when((line == 0) & (q > 0))
            def _():
                travel[token_rows(q), columns(c)] = sums[token_rows(q), columns(c)].astype(jnp.bfloat16)
                right_copy(q, c).start()

            @pl.when((line == far - 1) & (q < far - 1))
            def _():
                travel[token_rows(q), columns(c)] = sums[token_rows(q), columns(c)].astype(jnp.bfloat16)
                left_copy(q, c).start()

            return carry

        lax.fori_loop(0, far, block, 0)

    def pass_right(c):
        def block(k, carry):
            q = far - 1 - k
            right_copy(q, c).wait_recv()
            total = sums[token_rows(q), columns(c)] + travel[token_rows(q), columns(c)].astype(jnp.float32)
            travel[token_rows(q), columns(c)] = total.astype(jnp.bfloat16)
            right_copy(q, c).start()
            return carry

        lax.fori_loop(0, lax.select(line > 0, far - 1 - line, 0), block, 0)

    def pass_left(c):
        def block(q, carry):
            left_copy(q, c).wait_recv()
            total = sums[token_rows(q), columns(c)] + travel[token_rows(q), columns(c)].astype(jnp.float32)
            travel[token_rows(q), columns(c)] = total.astype(jnp.bfloat16)
            left_copy(q, c).start()
            return carry

        lax.fori_loop(0, lax.select(line < far - 1, line, 0), block, 0)

    def forward(c):
        @pl.when(line * 2 < far)
        def _():
            pass_right(c)
            pass_left(c)

        @pl.when(line * 2 >= far)
        def _():
            pass_left(c)
            pass_right(c)

    def step(c, carry):
        multiply(c)

        @pl.when(c > 0)
        def _():
            forward(c - 1)

        return carry

    lax.fori_loop(0, chunks, step, 0)
    forward(chunks - 1)

    def finish(c, carry):
        sums[token_rows(line), columns(c)] += resid[:, columns(c)].astype(jnp.float32)

        @pl.when(line > 0)
        def _():
            right_copy(line, c).wait_recv()
            sums[token_rows(line), columns(c)] += travel[token_rows(line), columns(c)].astype(jnp.float32)

        @pl.when(line < far - 1)
        def _():
            left_copy(line, c).wait_recv()
            sums[token_rows(line), columns(c)] += travel[token_rows(far), columns(c)].astype(jnp.float32)

        state = sums[token_rows(line), columns(c)].astype(jnp.bfloat16)
        hidden[:, columns(c)] = state
        state_float = state.astype(jnp.float32)
        square = state_float * state_float
        squares[0] += sum(square[:, k * 128 : (k + 1) * 128] for k in range(wide // 128))
        return carry

    squares[0] = jnp.zeros((rows, 128), jnp.float32)
    lax.fori_loop(0, chunks, finish, 0)

    square_copy = pltpu.make_async_remote_copy(
        src_ref=squares.at[0],
        dst_ref=squares.at[1],
        send_sem=square_send,
        recv_sem=square_recv,
        device_id={"tensor": 1 - side},
        device_id_type=pl.DeviceIdType.MESH,
    )
    square_copy.start()
    square_copy.wait()
    mean = jnp.sum(squares[0] + squares[1], axis=1, keepdims=True) / (2 * half)
    row_scale = lax.rsqrt(mean + epsilon)
    quarter = half // 2
    for c in range(chunks):
        at, of = c // (chunks // 2), c % (chunks // 2)
        here = slice(c * wide, (c + 1) * wide)
        normed = hidden[:, here].astype(jnp.float32) * row_scale * gain[pl.ds(side, 1), here]
        stacked[at * rows : (at + 1) * rows, of * wide : (of + 1) * wide] = normed.astype(jnp.bfloat16)

    both = pick.shape[0] // members
    cap = both // 2

    def slot_rows(e):
        return pl.ds(pl.multiple_of(e * both, both), both)

    def plane_rows(q, size):
        return pl.ds(pl.multiple_of(q * near * size, near * size), near * size)

    own_features = pltpu.make_async_copy(packed.at[slot_rows(me), :], features.at[side, slot_rows(me), :], own_sem.at[5])
    own_product = pltpu.make_async_copy(product.at[slot_rows(me), :], returned.at[slot_rows(me), :], own_sem.at[6])

    def row_copy(target, source):
        return pltpu.make_async_remote_copy(
            src_ref=packed.at[slot_rows(target), :],
            dst_ref=features.at[side, slot_rows(source), :],
            send_sem=row_send.at[target],
            recv_sem=row_recv.at[source],
            device_id={"expert": target},
            device_id_type=pl.DeviceIdType.MESH,
        )

    def pair_copy(q):
        place = features.at[side, plane_rows(q, both), :]
        return pltpu.make_async_remote_copy(
            src_ref=place,
            dst_ref=place,
            send_sem=pair_send.at[q],
            recv_sem=pair_recv.at[q],
            device_id={"tensor": 1 - side},
            device_id_type=pl.DeviceIdType.MESH,
        )

    def active_copy(q):
        place = active.at[plane_rows(q, cap), pl.ds(pl.multiple_of(side * ffe, ffe), ffe)]
        return pltpu.make_async_remote_copy(
            src_ref=place,
            dst_ref=place,
            send_sem=active_send.at[q],
            recv_sem=active_recv.at[q],
            device_id={"tensor": 1 - side},
            device_id_type=pl.DeviceIdType.MESH,
        )

    def back_copy(target, source):
        return pltpu.make_async_remote_copy(
            src_ref=product.at[slot_rows(target), :],
            dst_ref=returned.at[slot_rows(source), :],
            send_sem=back_send.at[target],
            recv_sem=back_recv.at[source],
            device_id={"expert": target},
            device_id_type=pl.DeviceIdType.MESH,
        )

    def near_first(k):
        return lax.select(line * 2 < far, k, far - 1 - k)

    def dispatch(k, carry):
        q = near_first(far - 1 - k)
        packed[plane_rows(q, both), :] = jnp.dot(
            pick[plane_rows(q, both), :], stacked[...], preferred_element_type=jnp.float32
        ).astype(jnp.bfloat16)
        for j in range(near):
            target = q * near + j

            @pl.when(target != me)
            def _():
                row_copy(target, me).start()

            @pl.when(target == me)
            def _():
                own_features.start()

        return carry

    lax.fori_loop(0, far, dispatch, 0)
    for load in loads:
        load.wait()

    def expert_step(k, carry):
        @pl.when(k < far)
        def _():
            q = near_first(k)
            for j in range(near):
                source = q * near + j

                @pl.when(source != me)
                def _():
                    row_copy(source, source).wait_recv()

                @pl.when(source == me)
                def _():
                    own_features.wait()

            pair_copy(q).start()

        @pl.when((k >= 1) & (k < far + 1))
        def _():
            q = near_first(k - 1)
            pair_copy(q).wait_recv()
            parts = []
            for h in range(2):
                total = None
                for t in range(2):
                    first = t * half + h * quarter
                    term = jnp.dot(
                        features[t, plane_rows(q, both), :],
                        gate_up_local[first : first + quarter, :],
                        preferred_element_type=jnp.float32,
                    )
                    total = term if total is None else total + term
                parts.append(total)
            joined = jnp.concatenate(
                [
                    parts[0][j * both : j * both + cap] + parts[1][j * both + cap : (j + 1) * both]
                    for j in range(near)
                ],
                axis=0,
            )
            gate, up = joined[:, :ffe], joined[:, ffe:]
            active[plane_rows(q, cap), pl.ds(pl.multiple_of(side * ffe, ffe), ffe)] = (
                gate / (1.0 + jnp.exp(-gate)) * up
            ).astype(jnp.bfloat16)
            active_copy(q).start()

        @pl.when(k >= 2)
        def _():
            q = near_first(k - 2)
            active_copy(q).wait()
            out = jnp.dot(active[plane_rows(q, cap), :], down_local[...], preferred_element_type=jnp.float32)
            for j in range(near):
                target = q * near + j
                mine = out[j * cap : (j + 1) * cap]
                product[slot_rows(target), :] = jnp.concatenate(
                    [mine[:, :quarter], mine[:, quarter:]], axis=0
                ).astype(jnp.bfloat16)

                @pl.when(target != me)
                def _():
                    back_copy(target, me).start()

                @pl.when(target == me)
                def _():
                    own_product.start()

        return carry

    lax.fori_loop(0, far + 2, expert_step, 0)
    own_product.wait()

    def settle(d, carry):
        other = lax.rem(me + d, members)
        back_copy(other, other).wait_recv()
        back_copy(other, me).wait_send()
        row_copy(other, me).wait_send()
        return carry

    lax.fori_loop(1, members, settle, 0)
    for q in range(far):
        pair_copy(q).wait_send()

    for d in range(1, far):
        context_copy(d).wait_send()
        share_copy(d).wait_send()

    def drain(c, carry):
        for d in range(1, near):
            weight_copy(d, c).wait_send()

        def right_done(q, inner):
            right_copy(q, c).wait_send()
            return inner

        def left_done(q, inner):
            left_copy(q, c).wait_send()
            return inner

        lax.fori_loop(line + 1, far, right_done, 0)
        lax.fori_loop(0, line, left_done, 0)
        return carry

    lax.fori_loop(0, chunks, drain, 0)


def layer(resid, context, out_weight, gain, pick, gate_up, down_weight):
    members = lax.axis_size("expert")
    far = members // near
    rows, half = resid.shape
    depth = out_weight.shape[0]
    slot_rows = pick.shape[0]
    width, ffe = gate_up.shape[2:]
    dma = pltpu.SemaphoreType.DMA
    vmem = pl.BlockSpec(memory_space=pltpu.VMEM)
    far_spec = pl.BlockSpec(memory_space=pl.ANY)
    wire = jnp.bfloat16
    return pl.pallas_call(
        functools.partial(layer_kernel, members),
        out_shape=[
            jax.ShapeDtypeStruct((rows, half), wire),
            jax.ShapeDtypeStruct((slot_rows, half // 2), wire),
        ],
        in_specs=[vmem] * 5 + [far_spec] * 2,
        out_specs=[vmem, vmem],
        scratch_shapes=[
            pltpu.VMEM((near * depth, half), wire),
            pltpu.VMEM((far * rows, near * depth), wire),
            pltpu.VMEM((far * rows, half), jnp.float32),
            pltpu.VMEM(((far + 1) * rows, half), wire),
            pltpu.VMEM((2, rows, 128), jnp.float32),
            pltpu.VMEM((2 * rows, half // 2), wire),
            pltpu.VMEM((slot_rows, half // 2), wire),
            pltpu.VMEM((2, slot_rows, half // 2), wire),
            pltpu.VMEM((width, 2 * ffe), wire),
            pltpu.VMEM((2 * ffe, half), wire),
            pltpu.VMEM((slot_rows // 2, 2 * ffe), wire),
            pltpu.VMEM((slot_rows, half // 2), wire),
            dma((7,)),
            dma((near, chunks)),
            dma((near, chunks)),
            dma((far,)),
            dma((far,)),
            dma((far,)),
            dma((far,)),
            dma((far, chunks)),
            dma((far, chunks)),
            dma((far, chunks)),
            dma,
            dma,
            dma((members,)),
            dma((members,)),
            dma((far,)),
            dma((far,)),
            dma((far,)),
            dma((far,)),
            dma((members,)),
            dma((members,)),
        ],
        compiler_params=pltpu.CompilerParams(
            collective_id=0, has_side_effects=True, vmem_limit_bytes=60 * 2**20
        ),
        name="layer",
    )(resid, context, out_weight, gain, pick, gate_up, down_weight)


def per_device(
    resid,
    context,
    out_weight,
    norm_gain,
    gate_up,
    down_weight,
    expert_ids,
    slots,
    token_order,
    combine,
):
    tok_rows, half_width = resid.shape
    members, capacity = token_order.shape
    halves = jnp.arange(2, dtype=jnp.int32)
    tokens = jnp.arange(tok_rows, dtype=jnp.int32)
    pick = (token_order[:, None, :, None, None] == tokens) & (
        halves[None, :, None, None, None] == halves[None, None, None, :, None]
    )
    pick = pick.astype(jnp.bfloat16).reshape(members * 2 * capacity, 2 * tok_rows)
    hidden_state, table = layer(
        resid, context, out_weight, norm_gain.reshape(2, half_width), pick, gate_up, down_weight
    )
    flat_index = jnp.where(slots >= 0, (expert_ids * 2) * capacity + slots, -1)
    places = jnp.arange(members * 2 * capacity, dtype=jnp.int32)
    sums = []
    for h in range(2):
        weights = jnp.zeros((tok_rows, members * 2 * capacity), jnp.float32)
        for column in range(expert_ids.shape[1]):
            match = (flat_index[:, column, None] + h * capacity == places[None, :]) & (slots[:, column, None] >= 0)
            weights = weights + jnp.where(match, combine[:, column, None], 0.0)
        high = lax.reduce_precision(weights, 8, 7)
        low = lax.reduce_precision(weights - high, 8, 7)
        two = jnp.concatenate([high, low], axis=0).astype(jnp.bfloat16)
        total = jnp.dot(two, table, preferred_element_type=jnp.float32)
        sums.append(total[:tok_rows] + total[tok_rows:])
    mixed_sum = jnp.concatenate(sums, axis=1)
    return (hidden_state.astype(jnp.float32) + mixed_sum).astype(jnp.bfloat16)


def solution(mesh):
    placed = (
        P(("group", "expert"), "tensor"),
        P(("group", "expert"), None),
        P("expert", "tensor"),
        P(),
        P("expert", None, None, "tensor"),
        P("expert", None, "tensor"),
        P(("group", "expert"), None),
        P(("group", "expert"), None),
        P(("group", "expert"), None),
        P(("group", "expert"), None),
    )
    return jax.shard_map(
        per_device,
        mesh=mesh,
        in_specs=placed,
        out_specs=P(("group", "expert"), "tensor"),
        check_vma=False,
    )
```

```python
import functools

import jax
import jax.numpy as jnp
from jax import lax
from jax.experimental import pallas as pl
from jax.experimental.pallas import tpu as pltpu
from jax.sharding import PartitionSpec as P

epsilon = 1e-06
near = 4
chunks = 8


def layer_kernel(
    members,
    resid,
    context,
    weight,
    gain,
    order,
    expert_ids,
    slots,
    combine,
    gate_up,
    down_weight,
    mixed,
    plane_weight,
    line_context,
    sums,
    travel,
    squares,
    stacked,
    packed,
    features,
    gate_up_local,
    down_local,
    active,
    product,
    hidden,
    returned,
    pick,
    weights,
    own_sem,
    weight_send,
    weight_recv,
    context_send,
    context_recv,
    share_send,
    share_recv,
    chain_send,
    left_recv,
    right_recv,
    square_send,
    square_recv,
    row_send,
    row_recv,
    pair_send,
    pair_recv,
    active_send,
    active_recv,
    back_send,
    back_recv,
):
    far = members // near
    me = lax.axis_index("expert")
    side = lax.axis_index("tensor")
    line = lax.div(me, near)
    spot = lax.rem(me, near)
    rows, half = resid.shape
    depth = weight.shape[0]
    span = near * depth
    piece = span // 2
    wide = half // chunks

    def columns(c):
        return pl.ds(pl.multiple_of(c * wide, wide), wide)

    def token_rows(q):
        return pl.ds(pl.multiple_of(q * rows, rows), rows)

    own_columns = pl.ds(pl.multiple_of(side * piece, piece), piece)

    def weight_copy(d, c):
        slot = pl.ds(pl.multiple_of(spot * depth, depth), depth)
        return pltpu.make_async_remote_copy(
            src_ref=weight.at[:, columns(c)],
            dst_ref=plane_weight.at[slot, columns(c)],
            send_sem=weight_send.at[d, c],
            recv_sem=weight_recv.at[d, c],
            device_id={"expert": line * near + lax.bitwise_xor(spot, d)},
            device_id_type=pl.DeviceIdType.MESH,
        )

    def context_copy(d):
        target = lax.rem(line + d, far)
        return pltpu.make_async_remote_copy(
            src_ref=context.at[:, pl.ds(pl.multiple_of(target * span + side * piece, piece), piece)],
            dst_ref=line_context.at[token_rows(line), own_columns],
            send_sem=context_send.at[d],
            recv_sem=context_recv.at[d],
            device_id={"expert": target * near + spot},
            device_id_type=pl.DeviceIdType.MESH,
        )

    def share_copy(d):
        place = line_context.at[token_rows(lax.rem(line - d + far, far)), own_columns]
        return pltpu.make_async_remote_copy(
            src_ref=place,
            dst_ref=place,
            send_sem=share_send.at[d],
            recv_sem=share_recv.at[d],
            device_id={"tensor": 1 - side},
            device_id_type=pl.DeviceIdType.MESH,
        )

    def right_copy(q, c):
        return pltpu.make_async_remote_copy(
            src_ref=travel.at[token_rows(q), columns(c)],
            dst_ref=travel.at[token_rows(q), columns(c)],
            send_sem=chain_send.at[q, c],
            recv_sem=left_recv.at[q, c],
            device_id={"expert": me + near},
            device_id_type=pl.DeviceIdType.MESH,
        )

    def left_copy(q, c):
        return pltpu.make_async_remote_copy(
            src_ref=travel.at[token_rows(q), columns(c)],
            dst_ref=travel.at[token_rows(lax.select(q == line - 1, far, q)), columns(c)],
            send_sem=chain_send.at[q, c],
            recv_sem=right_recv.at[q, c],
            device_id={"expert": me - near},
            device_id_type=pl.DeviceIdType.MESH,
        )

    barrier = pltpu.get_barrier_semaphore()
    def greet(d, carry):
        pl.semaphore_signal(
            barrier,
            inc=1,
            device_id={"expert": lax.rem(me + d, members)},
            device_id_type=pl.DeviceIdType.MESH,
        )
        return carry

    lax.fori_loop(1, members, greet, 0)
    pl.semaphore_signal(barrier, inc=1, device_id={"tensor": 1 - side}, device_id_type=pl.DeviceIdType.MESH)
    own_weight = pltpu.make_async_copy(
        weight, plane_weight.at[pl.ds(pl.multiple_of(spot * depth, depth), depth), :], own_sem.at[0]
    )
    own_context = pltpu.make_async_copy(
        context.at[:, pl.ds(pl.multiple_of(line * span, span), span)],
        line_context.at[token_rows(line), :],
        own_sem.at[1],
    )
    own_weight.start()
    own_context.start()
    pl.semaphore_wait(barrier, members)

    for d in range(1, far):
        context_copy(d).start()
    for c in range(chunks):
        for d in (3, 1, 2):
            weight_copy(d, c).start()
    ffe = gate_up.shape[3]
    loads = [
        pltpu.make_async_copy(gate_up.at[0, 0], gate_up_local.at[:, :ffe], own_sem.at[2]),
        pltpu.make_async_copy(gate_up.at[0, 1], gate_up_local.at[:, ffe:], own_sem.at[3]),
        pltpu.make_async_copy(down_weight.at[0], down_local, own_sem.at[4]),
    ]
    for load in loads:
        load.start()
    wanted = order[...]
    pick[...] = jnp.where(wanted == lax.broadcasted_iota(jnp.int32, pick.shape, 1), 1.0, 0.0).astype(jnp.bfloat16)
    own_weight.wait()
    own_context.wait()
    for d in range(1, far):
        context_copy(d).wait_recv()
        share_copy(d).start()

    def multiply(c):
        for d in range(1, near):
            weight_copy(d, c).wait_recv()

        def block(k, carry):
            q = lax.select(line * 2 < far, far - 1 - k, k)

            @pl.when((c == 0) & (q != line))
            def _():
                share_copy(lax.rem(line - q + far, far)).wait_recv()

            sums[token_rows(q), columns(c)] = jnp.dot(
                line_context[token_rows(q), :], plane_weight[:, columns(c)], preferred_element_type=jnp.float32
            )

            @pl.when((line == 0) & (q > 0))
            def _():
                travel[token_rows(q), columns(c)] = sums[token_rows(q), columns(c)].astype(jnp.bfloat16)
                right_copy(q, c).start()

            @pl.when((line == far - 1) & (q < far - 1))
            def _():
                travel[token_rows(q), columns(c)] = sums[token_rows(q), columns(c)].astype(jnp.bfloat16)
                left_copy(q, c).start()

            return carry

        lax.fori_loop(0, far, block, 0)

    def pass_right(c):
        def block(k, carry):
            q = far - 1 - k
            right_copy(q, c).wait_recv()
            total = sums[token_rows(q), columns(c)] + travel[token_rows(q), columns(c)].astype(jnp.float32)
            travel[token_rows(q), columns(c)] = total.astype(jnp.bfloat16)
            right_copy(q, c).start()
            return carry

        lax.fori_loop(0, lax.select(line > 0, far - 1 - line, 0), block, 0)

    def pass_left(c):
        def block(q, carry):
            left_copy(q, c).wait_recv()
            total = sums[token_rows(q), columns(c)] + travel[token_rows(q), columns(c)].astype(jnp.float32)
            travel[token_rows(q), columns(c)] = total.astype(jnp.bfloat16)
            left_copy(q, c).start()
            return carry

        lax.fori_loop(0, lax.select(line < far - 1, line, 0), block, 0)

    def forward(c):
        @pl.when(line * 2 < far)
        def _():
            pass_right(c)
            pass_left(c)

        @pl.when(line * 2 >= far)
        def _():
            pass_left(c)
            pass_right(c)

    def step(c, carry):
        multiply(c)

        @pl.when(c > 0)
        def _():
            forward(c - 1)

        return carry

    lax.fori_loop(0, chunks, step, 0)
    forward(chunks - 1)

    def finish(c, carry):
        sums[token_rows(line), columns(c)] += resid[:, columns(c)].astype(jnp.float32)

        @pl.when(line > 0)
        def _():
            right_copy(line, c).wait_recv()
            sums[token_rows(line), columns(c)] += travel[token_rows(line), columns(c)].astype(jnp.float32)

        @pl.when(line < far - 1)
        def _():
            left_copy(line, c).wait_recv()
            sums[token_rows(line), columns(c)] += travel[token_rows(far), columns(c)].astype(jnp.float32)

        state = sums[token_rows(line), columns(c)].astype(jnp.bfloat16)
        hidden[:, columns(c)] = state
        state_float = state.astype(jnp.float32)
        square = state_float * state_float
        squares[0] += sum(square[:, k * 128 : (k + 1) * 128] for k in range(wide // 128))
        return carry

    squares[0] = jnp.zeros((rows, 128), jnp.float32)
    lax.fori_loop(0, chunks, finish, 0)

    square_copy = pltpu.make_async_remote_copy(
        src_ref=squares.at[0],
        dst_ref=squares.at[1],
        send_sem=square_send,
        recv_sem=square_recv,
        device_id={"tensor": 1 - side},
        device_id_type=pl.DeviceIdType.MESH,
    )
    square_copy.start()
    square_copy.wait()
    mean = jnp.sum(squares[0] + squares[1], axis=1, keepdims=True) / (2 * half)
    row_scale = lax.rsqrt(mean + epsilon)
    quarter = half // 2
    for c in range(chunks):
        at, of = c // (chunks // 2), c % (chunks // 2)
        here = slice(c * wide, (c + 1) * wide)
        normed = hidden[:, here].astype(jnp.float32) * row_scale * gain[:, pl.ds(pl.multiple_of(side * half + c * wide, wide), wide)]
        stacked[at * rows : (at + 1) * rows, of * wide : (of + 1) * wide] = normed.astype(jnp.bfloat16)

    both = pick.shape[0] // members
    cap = both // 2

    def slot_rows(e):
        return pl.ds(pl.multiple_of(e * both, both), both)

    def plane_rows(q, size):
        return pl.ds(pl.multiple_of(q * near * size, near * size), near * size)

    own_features = pltpu.make_async_copy(packed.at[slot_rows(me), :], features.at[side, slot_rows(me), :], own_sem.at[5])
    own_product = pltpu.make_async_copy(product.at[slot_rows(me), :], returned.at[slot_rows(me), :], own_sem.at[6])

    def row_copy(target, source):
        return pltpu.make_async_remote_copy(
            src_ref=packed.at[slot_rows(target), :],
            dst_ref=features.at[side, slot_rows(source), :],
            send_sem=row_send.at[target],
            recv_sem=row_recv.at[source],
            device_id={"expert": target},
            device_id_type=pl.DeviceIdType.MESH,
        )

    def pair_copy(q):
        place = features.at[side, plane_rows(q, both), :]
        return pltpu.make_async_remote_copy(
            src_ref=place,
            dst_ref=place,
            send_sem=pair_send.at[q],
            recv_sem=pair_recv.at[q],
            device_id={"tensor": 1 - side},
            device_id_type=pl.DeviceIdType.MESH,
        )

    def active_copy(q):
        place = active.at[plane_rows(q, cap), pl.ds(pl.multiple_of(side * ffe, ffe), ffe)]
        return pltpu.make_async_remote_copy(
            src_ref=place,
            dst_ref=place,
            send_sem=active_send.at[q],
            recv_sem=active_recv.at[q],
            device_id={"tensor": 1 - side},
            device_id_type=pl.DeviceIdType.MESH,
        )

    def back_copy(target, source):
        return pltpu.make_async_remote_copy(
            src_ref=product.at[slot_rows(target), :],
            dst_ref=returned.at[slot_rows(source), :],
            send_sem=back_send.at[target],
            recv_sem=back_recv.at[source],
            device_id={"expert": target},
            device_id_type=pl.DeviceIdType.MESH,
        )

    def near_first(k):
        return lax.select(line * 2 < far, k, far - 1 - k)

    def dispatch(k, carry):
        q = near_first(far - 1 - k)
        packed[plane_rows(q, both), :] = jnp.dot(
            pick[plane_rows(q, both), :], stacked[...], preferred_element_type=jnp.float32
        ).astype(jnp.bfloat16)
        for j in range(near):
            target = q * near + j

            @pl.when(target != me)
            def _():
                row_copy(target, me).start()

            @pl.when(target == me)
            def _():
                own_features.start()

        return carry

    lax.fori_loop(0, far, dispatch, 0)
    def weigh(q, carry):
        flat = expert_ids[...] * both + slots[...] - q * near * both
        live = slots[...] >= 0
        share = jnp.where(live, combine[...], 0.0)
        for h in range(2):
            place = lax.broadcasted_iota(jnp.int32, (rows, near * both), 1) - h * cap
            total = jnp.zeros((rows, near * both), jnp.float32)
            for k in range(expert_ids.shape[1]):
                same = live[:, k : k + 1] & (flat[:, k : k + 1] == place)
                total = total + jnp.where(same, share[:, k : k + 1], 0.0)
            high = total.astype(jnp.bfloat16)
            weights[q, h, :rows, :] = high
            weights[q, h, rows:, :] = (total - high.astype(jnp.float32)).astype(jnp.bfloat16)
        return carry

    lax.fori_loop(0, far, weigh, 0)
    sums[:rows, :] = hidden[...].astype(jnp.float32)
    for load in loads:
        load.wait()

    def expert_step(k, carry):
        @pl.when(k < far)
        def _():
            q = near_first(k)
            for j in range(near):
                source = q * near + j

                @pl.when(source != me)
                def _():
                    row_copy(source, source).wait_recv()

                @pl.when(source == me)
                def _():
                    own_features.wait()

            pair_copy(q).start()

        @pl.when((k >= 1) & (k < far + 1))
        def _():
            q = near_first(k - 1)
            pair_copy(q).wait_recv()
            parts = []
            for h in range(2):
                total = None
                for t in range(2):
                    first = t * half + h * quarter
                    term = jnp.dot(
                        features[t, plane_rows(q, both), :],
                        gate_up_local[first : first + quarter, :],
                        preferred_element_type=jnp.float32,
                    )
                    total = term if total is None else total + term
                parts.append(total)
            joined = jnp.concatenate(
                [
                    parts[0][j * both : j * both + cap] + parts[1][j * both + cap : (j + 1) * both]
                    for j in range(near)
                ],
                axis=0,
            )
            gate, up = joined[:, :ffe], joined[:, ffe:]
            active[plane_rows(q, cap), pl.ds(pl.multiple_of(side * ffe, ffe), ffe)] = (
                gate / (1.0 + jnp.exp(-gate)) * up
            ).astype(jnp.bfloat16)
            active_copy(q).start()

        @pl.when(k >= 2)
        def _():
            q = near_first(k - 2)
            active_copy(q).wait()
            out = jnp.dot(active[plane_rows(q, cap), :], down_local[...], preferred_element_type=jnp.float32)
            for j in range(near):
                target = q * near + j
                mine = out[j * cap : (j + 1) * cap]
                product[slot_rows(target), :] = jnp.concatenate(
                    [mine[:, :quarter], mine[:, quarter:]], axis=0
                ).astype(jnp.bfloat16)

                @pl.when(target != me)
                def _():
                    back_copy(target, me).start()

                @pl.when(target == me)
                def _():
                    own_product.start()

        return carry

    lax.fori_loop(0, far + 2, expert_step, 0)

    def mix(k, carry):
        q = near_first(k)
        for j in range(near):
            source = q * near + j

            @pl.when(source != me)
            def _():
                back_copy(source, source).wait_recv()

            @pl.when(source == me)
            def _():
                own_product.wait()

        for h in range(2):
            both_parts = jnp.dot(
                weights[q, h], returned[plane_rows(q, both), :], preferred_element_type=jnp.float32
            )
            sums[:rows, h * quarter : (h + 1) * quarter] += both_parts[:rows] + both_parts[rows:]
        return carry

    lax.fori_loop(0, far, mix, 0)
    mixed[...] = sums[:rows, :].astype(jnp.bfloat16)

    def settle(d, carry):
        other = lax.rem(me + d, members)
        back_copy(other, me).wait_send()
        row_copy(other, me).wait_send()
        return carry

    lax.fori_loop(1, members, settle, 0)
    for q in range(far):
        pair_copy(q).wait_send()

    for d in range(1, far):
        context_copy(d).wait_send()
        share_copy(d).wait_send()

    def drain(c, carry):
        for d in range(1, near):
            weight_copy(d, c).wait_send()

        def right_done(q, inner):
            right_copy(q, c).wait_send()
            return inner

        def left_done(q, inner):
            left_copy(q, c).wait_send()
            return inner

        lax.fori_loop(line + 1, far, right_done, 0)
        lax.fori_loop(0, line, left_done, 0)
        return carry

    lax.fori_loop(0, chunks, drain, 0)


def layer(resid, context, out_weight, gain, order, expert_ids, slots, combine, gate_up, down_weight):
    members = lax.axis_size("expert")
    far = members // near
    rows, half = resid.shape
    depth = out_weight.shape[0]
    slot_rows = order.shape[0]
    width, ffe = gate_up.shape[2:]
    dma = pltpu.SemaphoreType.DMA
    vmem = pl.BlockSpec(memory_space=pltpu.VMEM)
    far_spec = pl.BlockSpec(memory_space=pl.ANY)
    wire = jnp.bfloat16
    return pl.pallas_call(
        functools.partial(layer_kernel, members),
        out_shape=jax.ShapeDtypeStruct((rows, half), wire),
        in_specs=[vmem] + [far_spec] * 2 + [vmem] * 5 + [far_spec] * 2,
        out_specs=vmem,
        scratch_shapes=[
            pltpu.VMEM((near * depth, half), wire),
            pltpu.VMEM((far * rows, near * depth), wire),
            pltpu.VMEM((far * rows, half), jnp.float32),
            pltpu.VMEM(((far + 1) * rows, half), wire),
            pltpu.VMEM((2, rows, 128), jnp.float32),
            pltpu.VMEM((2 * rows, half // 2), wire),
            pltpu.VMEM((slot_rows, half // 2), wire),
            pltpu.VMEM((2, slot_rows, half // 2), wire),
            pltpu.VMEM((width, 2 * ffe), wire),
            pltpu.VMEM((2 * ffe, half), wire),
            pltpu.VMEM((slot_rows // 2, 2 * ffe), wire),
            pltpu.VMEM((slot_rows, half // 2), wire),
            pltpu.VMEM((rows, half), wire),
            pltpu.VMEM((slot_rows, half // 2), wire),
            pltpu.VMEM((slot_rows, 2 * rows), wire),
            pltpu.VMEM((far, 2, 2 * rows, slot_rows // far), wire),
            dma((7,)),
            dma((near, chunks)),
            dma((near, chunks)),
            dma((far,)),
            dma((far,)),
            dma((far,)),
            dma((far,)),
            dma((far, chunks)),
            dma((far, chunks)),
            dma((far, chunks)),
            dma,
            dma,
            dma((members,)),
            dma((members,)),
            dma((far,)),
            dma((far,)),
            dma((far,)),
            dma((far,)),
            dma((members,)),
            dma((members,)),
        ],
        compiler_params=pltpu.CompilerParams(
            collective_id=0, has_side_effects=True, vmem_limit_bytes=60 * 2**20
        ),
        name="layer",
    )(resid, context, out_weight, gain, order, expert_ids, slots, combine, gate_up, down_weight)


def per_device(
    resid,
    context,
    out_weight,
    norm_gain,
    gate_up,
    down_weight,
    expert_ids,
    slots,
    token_order,
    combine,
):
    tok_rows, half_width = resid.shape
    members, capacity = token_order.shape
    halves = jnp.arange(2, dtype=jnp.int32)[None, :, None] * tok_rows
    order = jnp.where(token_order[:, None, :] >= 0, token_order[:, None, :] + halves, -1)
    return layer(
        resid,
        context,
        out_weight,
        norm_gain.reshape(1, 2 * half_width),
        order.reshape(members * 2 * capacity, 1),
        expert_ids,
        slots,
        combine,
        gate_up,
        down_weight,
    )


def solution(mesh):
    placed = (
        P(("group", "expert"), "tensor"),
        P(("group", "expert"), None),
        P("expert", "tensor"),
        P(),
        P("expert", None, None, "tensor"),
        P("expert", None, "tensor"),
        P(("group", "expert"), None),
        P(("group", "expert"), None),
        P(("group", "expert"), None),
        P(("group", "expert"), None),
    )
    return jax.shard_map(
        per_device,
        mesh=mesh,
        in_specs=placed,
        out_specs=P(("group", "expert"), "tensor"),
        check_vma=False,
    )
```

```python
import functools

import jax
import jax.numpy as jnp
from jax import lax
from jax.experimental import pallas as pl
from jax.experimental.pallas import tpu as pltpu
from jax.sharding import PartitionSpec as P

epsilon = 1e-06
near = 4
chunks = 8


def layer_kernel(
    members,
    resid,
    context,
    weight,
    gain,
    order,
    choices,
    gate_up,
    down_weight,
    mixed,
    plane_weight,
    line_context,
    sums,
    travel,
    squares,
    stacked,
    packed,
    features,
    gate_up_local,
    down_local,
    active,
    product,
    hidden,
    returned,
    pick,
    weights,
    own_sem,
    weight_send,
    weight_recv,
    context_send,
    context_recv,
    share_send,
    share_recv,
    chain_send,
    left_recv,
    right_recv,
    square_send,
    square_recv,
    row_send,
    row_recv,
    pair_send,
    pair_recv,
    active_send,
    active_recv,
    back_send,
    back_recv,
):
    far = members // near
    me = lax.axis_index("expert")
    side = lax.axis_index("tensor")
    line = lax.div(me, near)
    spot = lax.rem(me, near)
    rows, half = resid.shape
    depth = weight.shape[0]
    span = near * depth
    piece = span // 2
    wide = half // chunks

    def columns(c):
        return pl.ds(pl.multiple_of(c * wide, wide), wide)

    def token_rows(q):
        return pl.ds(pl.multiple_of(q * rows, rows), rows)

    own_columns = pl.ds(pl.multiple_of(side * piece, piece), piece)

    def weight_copy(d, c):
        slot = pl.ds(pl.multiple_of(spot * depth, depth), depth)
        return pltpu.make_async_remote_copy(
            src_ref=weight.at[:, columns(c)],
            dst_ref=plane_weight.at[slot, columns(c)],
            send_sem=weight_send.at[d, c],
            recv_sem=weight_recv.at[d, c],
            device_id={"expert": line * near + lax.bitwise_xor(spot, d)},
            device_id_type=pl.DeviceIdType.MESH,
        )

    def corner_copy(c):
        d = 1 + lax.rem(c, 2)
        owner = lax.bitwise_xor(spot, 3 - d)
        place = plane_weight.at[pl.ds(pl.multiple_of(owner * depth, depth), depth), columns(c)]
        return pltpu.make_async_remote_copy(
            src_ref=place,
            dst_ref=place,
            send_sem=weight_send.at[3, c],
            recv_sem=weight_recv.at[3, c],
            device_id={"expert": line * near + lax.bitwise_xor(spot, d)},
            device_id_type=pl.DeviceIdType.MESH,
        )

    def hand_on(c):
        weight_copy(1, c).wait_recv()
        weight_copy(2, c).wait_recv()
        corner_copy(c).start()

    def context_copy(d):
        target = lax.rem(line + d, far)
        return pltpu.make_async_remote_copy(
            src_ref=context.at[:, pl.ds(pl.multiple_of(target * span + side * piece, piece), piece)],
            dst_ref=line_context.at[token_rows(line), own_columns],
            send_sem=context_send.at[d],
            recv_sem=context_recv.at[d],
            device_id={"expert": target * near + spot},
            device_id_type=pl.DeviceIdType.MESH,
        )

    def share_copy(d):
        place = line_context.at[token_rows(lax.rem(line - d + far, far)), own_columns]
        return pltpu.make_async_remote_copy(
            src_ref=place,
            dst_ref=place,
            send_sem=share_send.at[d],
            recv_sem=share_recv.at[d],
            device_id={"tensor": 1 - side},
            device_id_type=pl.DeviceIdType.MESH,
        )

    def right_copy(q, c):
        return pltpu.make_async_remote_copy(
            src_ref=travel.at[token_rows(q), columns(c)],
            dst_ref=travel.at[token_rows(q), columns(c)],
            send_sem=chain_send.at[q, c],
            recv_sem=left_recv.at[q, c],
            device_id={"expert": me + near},
            device_id_type=pl.DeviceIdType.MESH,
        )

    def left_copy(q, c):
        return pltpu.make_async_remote_copy(
            src_ref=travel.at[token_rows(q), columns(c)],
            dst_ref=travel.at[token_rows(lax.select(q == line - 1, far, q)), columns(c)],
            send_sem=chain_send.at[q, c],
            recv_sem=right_recv.at[q, c],
            device_id={"expert": me - near},
            device_id_type=pl.DeviceIdType.MESH,
        )

    barrier = pltpu.get_barrier_semaphore()
    def greet(d, carry):
        pl.semaphore_signal(
            barrier,
            inc=1,
            device_id={"expert": lax.rem(me + d, members)},
            device_id_type=pl.DeviceIdType.MESH,
        )
        return carry

    lax.fori_loop(1, members, greet, 0)
    pl.semaphore_signal(barrier, inc=1, device_id={"tensor": 1 - side}, device_id_type=pl.DeviceIdType.MESH)
    own_weight = pltpu.make_async_copy(
        weight, plane_weight.at[pl.ds(pl.multiple_of(spot * depth, depth), depth), :], own_sem.at[0]
    )
    own_context = pltpu.make_async_copy(
        context.at[:, pl.ds(pl.multiple_of(line * span, span), span)],
        line_context.at[token_rows(line), :],
        own_sem.at[1],
    )
    own_weight.start()
    own_context.start()
    pl.semaphore_wait(barrier, members)

    for d in range(1, far):
        context_copy(d).start()
    for c in range(chunks):
        for d in (1, 2):
            weight_copy(d, c).start()
    ffe = gate_up.shape[3]
    loads = [
        pltpu.make_async_copy(gate_up.at[0, 0], gate_up_local.at[:, :ffe], own_sem.at[2]),
        pltpu.make_async_copy(gate_up.at[0, 1], gate_up_local.at[:, ffe:], own_sem.at[3]),
        pltpu.make_async_copy(down_weight.at[0], down_local, own_sem.at[4]),
    ]
    for load in loads:
        load.start()
    wanted = order[...]
    pick[...] = jnp.where(wanted == lax.broadcasted_iota(jnp.int32, pick.shape, 1), 1.0, 0.0).astype(jnp.bfloat16)
    own_weight.wait()
    own_context.wait()
    for d in range(1, far):
        context_copy(d).wait_recv()
        share_copy(d).start()

    def multiply(c):
        @pl.when(c + 1 < chunks)
        def _():
            hand_on(c + 1)

        corner_copy(c).wait_recv()

        def block(k, carry):
            q = lax.select(line * 2 < far, far - 1 - k, k)

            @pl.when((c == 0) & (q != line))
            def _():
                share_copy(lax.rem(line - q + far, far)).wait_recv()

            sums[token_rows(q), columns(c)] = jnp.dot(
                line_context[token_rows(q), :], plane_weight[:, columns(c)], preferred_element_type=jnp.float32
            )

            @pl.when((line == 0) & (q > 0))
            def _():
                travel[token_rows(q), columns(c)] = sums[token_rows(q), columns(c)].astype(jnp.bfloat16)
                right_copy(q, c).start()

            @pl.when((line == far - 1) & (q < far - 1))
            def _():
                travel[token_rows(q), columns(c)] = sums[token_rows(q), columns(c)].astype(jnp.bfloat16)
                left_copy(q, c).start()

            return carry

        lax.fori_loop(0, far, block, 0)

    def pass_right(c):
        def block(k, carry):
            q = far - 1 - k
            right_copy(q, c).wait_recv()
            total = sums[token_rows(q), columns(c)] + travel[token_rows(q), columns(c)].astype(jnp.float32)
            travel[token_rows(q), columns(c)] = total.astype(jnp.bfloat16)
            right_copy(q, c).start()
            return carry

        lax.fori_loop(0, lax.select(line > 0, far - 1 - line, 0), block, 0)

    def pass_left(c):
        def block(q, carry):
            left_copy(q, c).wait_recv()
            total = sums[token_rows(q), columns(c)] + travel[token_rows(q), columns(c)].astype(jnp.float32)
            travel[token_rows(q), columns(c)] = total.astype(jnp.bfloat16)
            left_copy(q, c).start()
            return carry

        lax.fori_loop(0, lax.select(line < far - 1, line, 0), block, 0)

    def forward(c):
        @pl.when(line * 2 < far)
        def _():
            pass_right(c)
            pass_left(c)

        @pl.when(line * 2 >= far)
        def _():
            pass_left(c)
            pass_right(c)

    def step(c, carry):
        multiply(c)

        @pl.when(c > 0)
        def _():
            forward(c - 1)

        return carry

    hand_on(0)
    lax.fori_loop(0, chunks, step, 0)
    forward(chunks - 1)

    def finish(c, carry):
        sums[token_rows(line), columns(c)] += resid[:, columns(c)].astype(jnp.float32)

        @pl.when(line > 0)
        def _():
            right_copy(line, c).wait_recv()
            sums[token_rows(line), columns(c)] += travel[token_rows(line), columns(c)].astype(jnp.float32)

        @pl.when(line < far - 1)
        def _():
            left_copy(line, c).wait_recv()
            sums[token_rows(line), columns(c)] += travel[token_rows(far), columns(c)].astype(jnp.float32)

        state = sums[token_rows(line), columns(c)].astype(jnp.bfloat16)
        hidden[:, columns(c)] = state
        state_float = state.astype(jnp.float32)
        square = state_float * state_float
        squares[0] += sum(square[:, k * 128 : (k + 1) * 128] for k in range(wide // 128))
        return carry

    squares[0] = jnp.zeros((rows, 128), jnp.float32)
    lax.fori_loop(0, chunks, finish, 0)

    square_copy = pltpu.make_async_remote_copy(
        src_ref=squares.at[0],
        dst_ref=squares.at[1],
        send_sem=square_send,
        recv_sem=square_recv,
        device_id={"tensor": 1 - side},
        device_id_type=pl.DeviceIdType.MESH,
    )
    square_copy.start()
    square_copy.wait()
    mean = jnp.sum(squares[0] + squares[1], axis=1, keepdims=True) / (2 * half)
    row_scale = lax.rsqrt(mean + epsilon)
    quarter = half // 2
    for c in range(chunks):
        at, of = c // (chunks // 2), c % (chunks // 2)
        here = slice(c * wide, (c + 1) * wide)
        normed = hidden[:, here].astype(jnp.float32) * row_scale * gain[:, pl.ds(pl.multiple_of(side * half + c * wide, wide), wide)]
        stacked[at * rows : (at + 1) * rows, of * wide : (of + 1) * wide] = normed.astype(jnp.bfloat16)

    both = pick.shape[0] // members
    cap = both // 2

    def slot_rows(e):
        return pl.ds(pl.multiple_of(e * both, both), both)

    def plane_rows(q, size):
        return pl.ds(pl.multiple_of(q * near * size, near * size), near * size)

    own_features = pltpu.make_async_copy(packed.at[slot_rows(me), :], features.at[side, slot_rows(me), :], own_sem.at[5])
    own_product = pltpu.make_async_copy(product.at[slot_rows(me), :], returned.at[slot_rows(me), :], own_sem.at[6])

    def row_copy(target, source):
        return pltpu.make_async_remote_copy(
            src_ref=packed.at[slot_rows(target), :],
            dst_ref=features.at[side, slot_rows(source), :],
            send_sem=row_send.at[target],
            recv_sem=row_recv.at[source],
            device_id={"expert": target},
            device_id_type=pl.DeviceIdType.MESH,
        )

    def pair_copy(q):
        place = features.at[side, plane_rows(q, both), :]
        return pltpu.make_async_remote_copy(
            src_ref=place,
            dst_ref=place,
            send_sem=pair_send.at[q],
            recv_sem=pair_recv.at[q],
            device_id={"tensor": 1 - side},
            device_id_type=pl.DeviceIdType.MESH,
        )

    def active_copy(q):
        place = active.at[plane_rows(q, cap), pl.ds(pl.multiple_of(side * ffe, ffe), ffe)]
        return pltpu.make_async_remote_copy(
            src_ref=place,
            dst_ref=place,
            send_sem=active_send.at[q],
            recv_sem=active_recv.at[q],
            device_id={"tensor": 1 - side},
            device_id_type=pl.DeviceIdType.MESH,
        )

    def back_copy(target, source):
        return pltpu.make_async_remote_copy(
            src_ref=product.at[slot_rows(target), :],
            dst_ref=returned.at[slot_rows(source), :],
            send_sem=back_send.at[target],
            recv_sem=back_recv.at[source],
            device_id={"expert": target},
            device_id_type=pl.DeviceIdType.MESH,
        )

    def near_first(k):
        return lax.select(line * 2 < far, k, far - 1 - k)

    def dispatch(k, carry):
        q = near_first(far - 1 - k)
        packed[plane_rows(q, both), :] = jnp.dot(
            pick[plane_rows(q, both), :], stacked[...], preferred_element_type=jnp.float32
        ).astype(jnp.bfloat16)
        for j in range(near):
            target = q * near + j

            @pl.when(target != me)
            def _():
                row_copy(target, me).start()

            @pl.when(target == me)
            def _():
                own_features.start()

        return carry

    lax.fori_loop(0, far, dispatch, 0)
    def weigh(q, carry):
        top = choices.shape[1] // 2
        flat = choices[:, :top].astype(jnp.int32)
        live = flat >= 0
        flat = flat - q * near * both
        share = choices[:, top:]
        for h in range(2):
            place = lax.broadcasted_iota(jnp.int32, (rows, near * both), 1) - h * cap
            total = jnp.zeros((rows, near * both), jnp.float32)
            for k in range(top):
                same = live[:, k : k + 1] & (flat[:, k : k + 1] == place)
                total = total + jnp.where(same, share[:, k : k + 1], 0.0)
            high = total.astype(jnp.bfloat16)
            weights[q, h, :rows, :] = high
            weights[q, h, rows:, :] = (total - high.astype(jnp.float32)).astype(jnp.bfloat16)
        return carry

    lax.fori_loop(0, far, weigh, 0)
    sums[:rows, :] = hidden[...].astype(jnp.float32)
    for load in loads:
        load.wait()

    def expert_step(k, carry):
        @pl.when(k < far)
        def _():
            q = near_first(k)
            for j in range(near):
                source = q * near + j

                @pl.when(source != me)
                def _():
                    row_copy(source, source).wait_recv()

                @pl.when(source == me)
                def _():
                    own_features.wait()

            pair_copy(q).start()

        @pl.when((k >= 1) & (k < far + 1))
        def _():
            q = near_first(k - 1)
            pair_copy(q).wait_recv()
            parts = []
            for h in range(2):
                total = None
                for t in range(2):
                    first = t * half + h * quarter
                    term = jnp.dot(
                        features[t, plane_rows(q, both), :],
                        gate_up_local[first : first + quarter, :],
                        preferred_element_type=jnp.float32,
                    )
                    total = term if total is None else total + term
                parts.append(total)
            joined = jnp.concatenate(
                [
                    parts[0][j * both : j * both + cap] + parts[1][j * both + cap : (j + 1) * both]
                    for j in range(near)
                ],
                axis=0,
            )
            gate, up = joined[:, :ffe], joined[:, ffe:]
            active[plane_rows(q, cap), pl.ds(pl.multiple_of(side * ffe, ffe), ffe)] = (
                gate / (1.0 + jnp.exp(-gate)) * up
            ).astype(jnp.bfloat16)
            active_copy(q).start()

        @pl.when(k >= 2)
        def _():
            q = near_first(k - 2)
            active_copy(q).wait()
            out = jnp.dot(active[plane_rows(q, cap), :], down_local[...], preferred_element_type=jnp.float32)
            for j in range(near):
                target = q * near + j
                mine = out[j * cap : (j + 1) * cap]
                product[slot_rows(target), :] = jnp.concatenate(
                    [mine[:, :quarter], mine[:, quarter:]], axis=0
                ).astype(jnp.bfloat16)

                @pl.when(target != me)
                def _():
                    back_copy(target, me).start()

                @pl.when(target == me)
                def _():
                    own_product.start()

        return carry

    lax.fori_loop(0, far + 2, expert_step, 0)

    def mix(k, carry):
        q = near_first(k)
        for j in range(near):
            source = q * near + j

            @pl.when(source != me)
            def _():
                back_copy(source, source).wait_recv()

            @pl.when(source == me)
            def _():
                own_product.wait()

        for h in range(2):
            both_parts = jnp.dot(
                weights[q, h], returned[plane_rows(q, both), :], preferred_element_type=jnp.float32
            )
            sums[:rows, h * quarter : (h + 1) * quarter] += both_parts[:rows] + both_parts[rows:]
        return carry

    lax.fori_loop(0, far, mix, 0)
    mixed[...] = sums[:rows, :].astype(jnp.bfloat16)

    def settle(d, carry):
        other = lax.rem(me + d, members)
        back_copy(other, me).wait_send()
        row_copy(other, me).wait_send()
        return carry

    lax.fori_loop(1, members, settle, 0)
    for q in range(far):
        pair_copy(q).wait_send()

    for d in range(1, far):
        context_copy(d).wait_send()
        share_copy(d).wait_send()

    def drain(c, carry):
        for d in range(1, near - 1):
            weight_copy(d, c).wait_send()
        corner_copy(c).wait_send()

        def right_done(q, inner):
            right_copy(q, c).wait_send()
            return inner

        def left_done(q, inner):
            left_copy(q, c).wait_send()
            return inner

        lax.fori_loop(line + 1, far, right_done, 0)
        lax.fori_loop(0, line, left_done, 0)
        return carry

    lax.fori_loop(0, chunks, drain, 0)


def layer(resid, context, out_weight, gain, order, choices, gate_up, down_weight):
    members = lax.axis_size("expert")
    far = members // near
    rows, half = resid.shape
    depth = out_weight.shape[0]
    slot_rows = order.shape[0]
    width, ffe = gate_up.shape[2:]
    dma = pltpu.SemaphoreType.DMA
    vmem = pl.BlockSpec(memory_space=pltpu.VMEM)
    far_spec = pl.BlockSpec(memory_space=pl.ANY)
    wire = jnp.bfloat16
    return pl.pallas_call(
        functools.partial(layer_kernel, members),
        out_shape=jax.ShapeDtypeStruct((rows, half), wire),
        in_specs=[vmem] + [far_spec] * 2 + [vmem] * 3 + [far_spec] * 2,
        out_specs=vmem,
        scratch_shapes=[
            pltpu.VMEM((near * depth, half), wire),
            pltpu.VMEM((far * rows, near * depth), wire),
            pltpu.VMEM((far * rows, half), jnp.float32),
            pltpu.VMEM(((far + 1) * rows, half), wire),
            pltpu.VMEM((2, rows, 128), jnp.float32),
            pltpu.VMEM((2 * rows, half // 2), wire),
            pltpu.VMEM((slot_rows, half // 2), wire),
            pltpu.VMEM((2, slot_rows, half // 2), wire),
            pltpu.VMEM((width, 2 * ffe), wire),
            pltpu.VMEM((2 * ffe, half), wire),
            pltpu.VMEM((slot_rows // 2, 2 * ffe), wire),
            pltpu.VMEM((slot_rows, half // 2), wire),
            pltpu.VMEM((rows, half), wire),
            pltpu.VMEM((slot_rows, half // 2), wire),
            pltpu.VMEM((slot_rows, 2 * rows), wire),
            pltpu.VMEM((far, 2, 2 * rows, slot_rows // far), wire),
            dma((7,)),
            dma((near, chunks)),
            dma((near, chunks)),
            dma((far,)),
            dma((far,)),
            dma((far,)),
            dma((far,)),
            dma((far, chunks)),
            dma((far, chunks)),
            dma((far, chunks)),
            dma,
            dma,
            dma((members,)),
            dma((members,)),
            dma((far,)),
            dma((far,)),
            dma((far,)),
            dma((far,)),
            dma((members,)),
            dma((members,)),
        ],
        compiler_params=pltpu.CompilerParams(
            collective_id=0, has_side_effects=True, vmem_limit_bytes=60 * 2**20
        ),
        name="layer",
    )(resid, context, out_weight, gain, order, choices, gate_up, down_weight)


def per_device(
    resid,
    context,
    out_weight,
    norm_gain,
    gate_up,
    down_weight,
    expert_ids,
    slots,
    token_order,
    combine,
):
    tok_rows, half_width = resid.shape
    members, capacity = token_order.shape
    halves = jnp.arange(2, dtype=jnp.int32)[None, :, None] * tok_rows
    order = jnp.where(token_order[:, None, :] >= 0, token_order[:, None, :] + halves, -1)
    live = slots >= 0
    place = jnp.where(live, expert_ids * (2 * capacity) + slots, -1).astype(jnp.float32)
    choices = jnp.concatenate([place, jnp.where(live, combine, 0.0)], axis=1)
    return layer(
        resid,
        context,
        out_weight,
        norm_gain.reshape(1, 2 * half_width),
        order.reshape(members * 2 * capacity, 1),
        choices,
        gate_up,
        down_weight,
    )


def solution(mesh):
    placed = (
        P(("group", "expert"), "tensor"),
        P(("group", "expert"), None),
        P("expert", "tensor"),
        P(),
        P("expert", None, None, "tensor"),
        P("expert", None, "tensor"),
        P(("group", "expert"), None),
        P(("group", "expert"), None),
        P(("group", "expert"), None),
        P(("group", "expert"), None),
    )
    return jax.shard_map(
        per_device,
        mesh=mesh,
        in_specs=placed,
        out_specs=P(("group", "expert"), "tensor"),
        check_vma=False,
    )
```

```python
import functools

import jax
import jax.numpy as jnp
from jax import lax
from jax.experimental import pallas as pl
from jax.experimental.pallas import tpu as pltpu
from jax.sharding import PartitionSpec as P

epsilon = 1e-06
near = 4
chunks = 8


def layer_kernel(
    members,
    resid,
    context,
    weight,
    gain,
    order,
    choices,
    gate_up,
    down_weight,
    mixed,
    plane_weight,
    line_context,
    sums,
    travel,
    squares,
    stacked,
    packed,
    features,
    gate_up_local,
    down_local,
    active,
    product,
    hidden,
    returned,
    pick,
    weights,
    own_sem,
    weight_send,
    weight_recv,
    context_send,
    context_recv,
    share_send,
    share_recv,
    chain_send,
    left_recv,
    right_recv,
    square_send,
    square_recv,
    row_send,
    row_recv,
    pair_send,
    pair_recv,
    active_send,
    active_recv,
    back_send,
    back_recv,
):
    far = members // near
    me = lax.axis_index("expert")
    side = lax.axis_index("tensor")
    line = lax.div(me, near)
    spot = lax.rem(me, near)
    rows, half = resid.shape
    depth = weight.shape[0]
    span = near * depth
    piece = span // 2
    wide = half // chunks

    def columns(c):
        return pl.ds(pl.multiple_of(c * wide, wide), wide)

    def token_rows(q):
        return pl.ds(pl.multiple_of(q * rows, rows), rows)

    own_columns = pl.ds(pl.multiple_of(side * piece, piece), piece)

    def weight_copy(d, c):
        slot = pl.ds(pl.multiple_of(spot * depth, depth), depth)
        return pltpu.make_async_remote_copy(
            src_ref=weight.at[:, columns(c)],
            dst_ref=plane_weight.at[slot, columns(c)],
            send_sem=weight_send.at[d, c],
            recv_sem=weight_recv.at[d, c],
            device_id={"expert": line * near + lax.bitwise_xor(spot, d)},
            device_id_type=pl.DeviceIdType.MESH,
        )

    def context_copy(d):
        target = lax.rem(line + d, far)
        return pltpu.make_async_remote_copy(
            src_ref=context.at[:, pl.ds(pl.multiple_of(target * span + side * piece, piece), piece)],
            dst_ref=line_context.at[token_rows(line), own_columns],
            send_sem=context_send.at[d],
            recv_sem=context_recv.at[d],
            device_id={"expert": target * near + spot},
            device_id_type=pl.DeviceIdType.MESH,
        )

    def share_copy(d):
        place = line_context.at[token_rows(lax.rem(line - d + far, far)), own_columns]
        return pltpu.make_async_remote_copy(
            src_ref=place,
            dst_ref=place,
            send_sem=share_send.at[d],
            recv_sem=share_recv.at[d],
            device_id={"tensor": 1 - side},
            device_id_type=pl.DeviceIdType.MESH,
        )

    def right_copy(q, c):
        return pltpu.make_async_remote_copy(
            src_ref=travel.at[token_rows(q), columns(c)],
            dst_ref=travel.at[token_rows(q), columns(c)],
            send_sem=chain_send.at[q, c],
            recv_sem=left_recv.at[q, c],
            device_id={"expert": me + near},
            device_id_type=pl.DeviceIdType.MESH,
        )

    def left_copy(q, c):
        return pltpu.make_async_remote_copy(
            src_ref=travel.at[token_rows(q), columns(c)],
            dst_ref=travel.at[token_rows(lax.select(q == line - 1, far, q)), columns(c)],
            send_sem=chain_send.at[q, c],
            recv_sem=right_recv.at[q, c],
            device_id={"expert": me - near},
            device_id_type=pl.DeviceIdType.MESH,
        )

    barrier = pltpu.get_barrier_semaphore()
    def greet(d, carry):
        pl.semaphore_signal(
            barrier,
            inc=1,
            device_id={"expert": lax.rem(me + d, members)},
            device_id_type=pl.DeviceIdType.MESH,
        )
        return carry

    lax.fori_loop(1, members, greet, 0)
    pl.semaphore_signal(barrier, inc=1, device_id={"tensor": 1 - side}, device_id_type=pl.DeviceIdType.MESH)
    own_weight = pltpu.make_async_copy(
        weight, plane_weight.at[pl.ds(pl.multiple_of(spot * depth, depth), depth), :], own_sem.at[0]
    )
    own_context = pltpu.make_async_copy(
        context.at[:, pl.ds(pl.multiple_of(line * span, span), span)],
        line_context.at[token_rows(line), :],
        own_sem.at[1],
    )
    own_weight.start()
    own_context.start()
    pl.semaphore_wait(barrier, members)

    for d in range(1, far):
        context_copy(d).start()
    for c in range(chunks):
        for d in (3, 1, 2):
            weight_copy(d, c).start()
    ffe = gate_up.shape[3]
    loads = [
        pltpu.make_async_copy(gate_up.at[0, 0], gate_up_local.at[:, :ffe], own_sem.at[2]),
        pltpu.make_async_copy(gate_up.at[0, 1], gate_up_local.at[:, ffe:], own_sem.at[3]),
        pltpu.make_async_copy(down_weight.at[0], down_local, own_sem.at[4]),
    ]
    for load in loads:
        load.start()
    wanted = order[...]
    pick[...] = jnp.where(wanted == lax.broadcasted_iota(jnp.int32, pick.shape, 1), 1.0, 0.0).astype(jnp.bfloat16)
    own_weight.wait()
    own_context.wait()
    for d in range(1, far):
        context_copy(d).wait_recv()
        share_copy(d).start()

    def multiply(c):
        for d in range(1, near):
            weight_copy(d, c).wait_recv()

        def block(k, carry):
            q = lax.select(line * 2 < far, far - 1 - k, k)

            @pl.when((c == 0) & (q != line))
            def _():
                share_copy(lax.rem(line - q + far, far)).wait_recv()

            sums[token_rows(q), columns(c)] = jnp.dot(
                line_context[token_rows(q), :], plane_weight[:, columns(c)], preferred_element_type=jnp.float32
            )

            @pl.when((line == 0) & (q > 0))
            def _():
                travel[token_rows(q), columns(c)] = sums[token_rows(q), columns(c)].astype(jnp.bfloat16)
                right_copy(q, c).start()

            @pl.when((line == far - 1) & (q < far - 1))
            def _():
                travel[token_rows(q), columns(c)] = sums[token_rows(q), columns(c)].astype(jnp.bfloat16)
                left_copy(q, c).start()

            return carry

        lax.fori_loop(0, far, block, 0)

    def pass_right(c):
        def block(k, carry):
            q = far - 1 - k
            right_copy(q, c).wait_recv()
            total = sums[token_rows(q), columns(c)] + travel[token_rows(q), columns(c)].astype(jnp.float32)
            travel[token_rows(q), columns(c)] = total.astype(jnp.bfloat16)
            right_copy(q, c).start()
            return carry

        lax.fori_loop(0, lax.select(line > 0, far - 1 - line, 0), block, 0)

    def pass_left(c):
        def block(q, carry):
            left_copy(q, c).wait_recv()
            total = sums[token_rows(q), columns(c)] + travel[token_rows(q), columns(c)].astype(jnp.float32)
            travel[token_rows(q), columns(c)] = total.astype(jnp.bfloat16)
            left_copy(q, c).start()
            return carry

        lax.fori_loop(0, lax.select(line < far - 1, line, 0), block, 0)

    def forward(c):
        @pl.when(line * 2 < far)
        def _():
            pass_right(c)
            pass_left(c)

        @pl.when(line * 2 >= far)
        def _():
            pass_left(c)
            pass_right(c)

    def step(c, carry):
        multiply(c)

        @pl.when(c > 0)
        def _():
            forward(c - 1)

        return carry

    lax.fori_loop(0, chunks, step, 0)
    forward(chunks - 1)

    def finish(c, carry):
        sums[token_rows(line), columns(c)] += resid[:, columns(c)].astype(jnp.float32)

        @pl.when(line > 0)
        def _():
            right_copy(line, c).wait_recv()
            sums[token_rows(line), columns(c)] += travel[token_rows(line), columns(c)].astype(jnp.float32)

        @pl.when(line < far - 1)
        def _():
            left_copy(line, c).wait_recv()
            sums[token_rows(line), columns(c)] += travel[token_rows(far), columns(c)].astype(jnp.float32)

        state = sums[token_rows(line), columns(c)].astype(jnp.bfloat16)
        hidden[:, columns(c)] = state
        state_float = state.astype(jnp.float32)
        square = state_float * state_float
        squares[0] += sum(square[:, k * 128 : (k + 1) * 128] for k in range(wide // 128))
        return carry

    squares[0] = jnp.zeros((rows, 128), jnp.float32)
    lax.fori_loop(0, chunks, finish, 0)

    square_copy = pltpu.make_async_remote_copy(
        src_ref=squares.at[0],
        dst_ref=squares.at[1],
        send_sem=square_send,
        recv_sem=square_recv,
        device_id={"tensor": 1 - side},
        device_id_type=pl.DeviceIdType.MESH,
    )
    square_copy.start()
    square_copy.wait()
    mean = jnp.sum(squares[0] + squares[1], axis=1, keepdims=True) / (2 * half)
    row_scale = lax.rsqrt(mean + epsilon)
    quarter = half // 2
    for c in range(chunks):
        at, of = c // (chunks // 2), c % (chunks // 2)
        here = slice(c * wide, (c + 1) * wide)
        normed = hidden[:, here].astype(jnp.float32) * row_scale * gain[:, pl.ds(pl.multiple_of(side * half + c * wide, wide), wide)]
        stacked[at * rows : (at + 1) * rows, of * wide : (of + 1) * wide] = normed.astype(jnp.bfloat16)

    both = pick.shape[0] // members
    cap = both // 2

    def slot_rows(e):
        return pl.ds(pl.multiple_of(e * both, both), both)

    def plane_rows(q, size):
        return pl.ds(pl.multiple_of(q * near * size, near * size), near * size)

    own_features = pltpu.make_async_copy(packed.at[slot_rows(me), :], features.at[side, slot_rows(me), :], own_sem.at[5])
    own_product = pltpu.make_async_copy(product.at[slot_rows(me), :], returned.at[slot_rows(me), :], own_sem.at[6])

    def row_copy(target, source):
        return pltpu.make_async_remote_copy(
            src_ref=packed.at[slot_rows(target), :],
            dst_ref=features.at[side, slot_rows(source), :],
            send_sem=row_send.at[target],
            recv_sem=row_recv.at[source],
            device_id={"expert": target},
            device_id_type=pl.DeviceIdType.MESH,
        )

    def pair_copy(q):
        place = features.at[side, plane_rows(q, both), :]
        return pltpu.make_async_remote_copy(
            src_ref=place,
            dst_ref=place,
            send_sem=pair_send.at[q],
            recv_sem=pair_recv.at[q],
            device_id={"tensor": 1 - side},
            device_id_type=pl.DeviceIdType.MESH,
        )

    def active_copy(q):
        place = active.at[plane_rows(q, cap), pl.ds(pl.multiple_of(side * ffe, ffe), ffe)]
        return pltpu.make_async_remote_copy(
            src_ref=place,
            dst_ref=place,
            send_sem=active_send.at[q],
            recv_sem=active_recv.at[q],
            device_id={"tensor": 1 - side},
            device_id_type=pl.DeviceIdType.MESH,
        )

    def back_copy(target, source):
        return pltpu.make_async_remote_copy(
            src_ref=product.at[slot_rows(target), :],
            dst_ref=returned.at[slot_rows(source), :],
            send_sem=back_send.at[target],
            recv_sem=back_recv.at[source],
            device_id={"expert": target},
            device_id_type=pl.DeviceIdType.MESH,
        )

    def near_first(k):
        return lax.select(line * 2 < far, k, far - 1 - k)

    def dispatch(k, carry):
        q = near_first(far - 1 - k)
        packed[plane_rows(q, both), :] = jnp.dot(
            pick[plane_rows(q, both), :], stacked[...], preferred_element_type=jnp.float32
        ).astype(jnp.bfloat16)
        for j in range(near):
            target = q * near + j

            @pl.when(target != me)
            def _():
                row_copy(target, me).start()

            @pl.when(target == me)
            def _():
                own_features.start()

        return carry

    lax.fori_loop(0, far, dispatch, 0)
    def weigh(q, carry):
        top = choices.shape[1] // 2
        flat = choices[:, :top].astype(jnp.int32)
        live = flat >= 0
        flat = flat - q * near * both
        share = choices[:, top:]
        for h in range(2):
            place = lax.broadcasted_iota(jnp.int32, (rows, near * both), 1) - h * cap
            total = jnp.zeros((rows, near * both), jnp.float32)
            for k in range(top):
                same = live[:, k : k + 1] & (flat[:, k : k + 1] == place)
                total = total + jnp.where(same, share[:, k : k + 1], 0.0)
            high = total.astype(jnp.bfloat16)
            weights[q, h, :rows, :] = high
            weights[q, h, rows:, :] = (total - high.astype(jnp.float32)).astype(jnp.bfloat16)
        return carry

    lax.fori_loop(0, far, weigh, 0)
    sums[:rows, :] = hidden[...].astype(jnp.float32)
    for load in loads:
        load.wait()

    def expert_step(k, carry):
        @pl.when(k < far)
        def _():
            q = near_first(k)
            for j in range(near):
                source = q * near + j

                @pl.when(source != me)
                def _():
                    row_copy(source, source).wait_recv()

                @pl.when(source == me)
                def _():
                    own_features.wait()

            pair_copy(q).start()

        @pl.when((k >= 1) & (k < far + 1))
        def _():
            q = near_first(k - 1)
            pair_copy(q).wait_recv()
            parts = []
            for h in range(2):
                total = None
                for t in range(2):
                    first = t * half + h * quarter
                    term = jnp.dot(
                        features[t, plane_rows(q, both), :],
                        gate_up_local[first : first + quarter, :],
                        preferred_element_type=jnp.float32,
                    )
                    total = term if total is None else total + term
                parts.append(total)
            joined = jnp.concatenate(
                [
                    parts[0][j * both : j * both + cap] + parts[1][j * both + cap : (j + 1) * both]
                    for j in range(near)
                ],
                axis=0,
            )
            gate, up = joined[:, :ffe], joined[:, ffe:]
            active[plane_rows(q, cap), pl.ds(pl.multiple_of(side * ffe, ffe), ffe)] = (
                gate / (1.0 + jnp.exp(-gate)) * up
            ).astype(jnp.bfloat16)
            active_copy(q).start()

        @pl.when(k >= 2)
        def _():
            q = near_first(k - 2)
            active_copy(q).wait()
            out = jnp.dot(active[plane_rows(q, cap), :], down_local[...], preferred_element_type=jnp.float32)
            for j in range(near):
                target = q * near + j
                mine = out[j * cap : (j + 1) * cap]
                product[slot_rows(target), :] = jnp.concatenate(
                    [mine[:, :quarter], mine[:, quarter:]], axis=0
                ).astype(jnp.bfloat16)

                @pl.when(target != me)
                def _():
                    back_copy(target, me).start()

                @pl.when(target == me)
                def _():
                    own_product.start()

        return carry

    lax.fori_loop(0, far + 2, expert_step, 0)

    def mix(k, carry):
        q = near_first(k)
        for j in range(near):
            source = q * near + j

            @pl.when(source != me)
            def _():
                back_copy(source, source).wait_recv()

            @pl.when(source == me)
            def _():
                own_product.wait()

        for h in range(2):
            both_parts = jnp.dot(
                weights[q, h], returned[plane_rows(q, both), :], preferred_element_type=jnp.float32
            )
            sums[:rows, h * quarter : (h + 1) * quarter] += both_parts[:rows] + both_parts[rows:]
        return carry

    lax.fori_loop(0, far, mix, 0)
    mixed[...] = sums[:rows, :].astype(jnp.bfloat16)

    def settle(d, carry):
        other = lax.rem(me + d, members)
        back_copy(other, me).wait_send()
        row_copy(other, me).wait_send()
        return carry

    lax.fori_loop(1, members, settle, 0)
    for q in range(far):
        pair_copy(q).wait_send()

    for d in range(1, far):
        context_copy(d).wait_send()
        share_copy(d).wait_send()

    def drain(c, carry):
        for d in range(1, near):
            weight_copy(d, c).wait_send()

        def right_done(q, inner):
            right_copy(q, c).wait_send()
            return inner

        def left_done(q, inner):
            left_copy(q, c).wait_send()
            return inner

        lax.fori_loop(line + 1, far, right_done, 0)
        lax.fori_loop(0, line, left_done, 0)
        return carry

    lax.fori_loop(0, chunks, drain, 0)


def layer(resid, context, out_weight, gain, order, choices, gate_up, down_weight):
    members = lax.axis_size("expert")
    far = members // near
    rows, half = resid.shape
    depth = out_weight.shape[0]
    slot_rows = order.shape[0]
    width, ffe = gate_up.shape[2:]
    dma = pltpu.SemaphoreType.DMA
    vmem = pl.BlockSpec(memory_space=pltpu.VMEM)
    far_spec = pl.BlockSpec(memory_space=pl.ANY)
    wire = jnp.bfloat16
    return pl.pallas_call(
        functools.partial(layer_kernel, members),
        out_shape=jax.ShapeDtypeStruct((rows, half), wire),
        in_specs=[vmem] + [far_spec] * 2 + [vmem] * 3 + [far_spec] * 2,
        out_specs=vmem,
        scratch_shapes=[
            pltpu.VMEM((near * depth, half), wire),
            pltpu.VMEM((far * rows, near * depth), wire),
            pltpu.VMEM((far * rows, half), jnp.float32),
            pltpu.VMEM(((far + 1) * rows, half), wire),
            pltpu.VMEM((2, rows, 128), jnp.float32),
            pltpu.VMEM((2 * rows, half // 2), wire),
            pltpu.VMEM((slot_rows, half // 2), wire),
            pltpu.VMEM((2, slot_rows, half // 2), wire),
            pltpu.VMEM((width, 2 * ffe), wire),
            pltpu.VMEM((2 * ffe, half), wire),
            pltpu.VMEM((slot_rows // 2, 2 * ffe), wire),
            pltpu.VMEM((slot_rows, half // 2), wire),
            pltpu.VMEM((rows, half), wire),
            pltpu.VMEM((slot_rows, half // 2), wire),
            pltpu.VMEM((slot_rows, 2 * rows), wire),
            pltpu.VMEM((far, 2, 2 * rows, slot_rows // far), wire),
            dma((7,)),
            dma((near, chunks)),
            dma((near, chunks)),
            dma((far,)),
            dma((far,)),
            dma((far,)),
            dma((far,)),
            dma((far, chunks)),
            dma((far, chunks)),
            dma((far, chunks)),
            dma,
            dma,
            dma((members,)),
            dma((members,)),
            dma((far,)),
            dma((far,)),
            dma((far,)),
            dma((far,)),
            dma((members,)),
            dma((members,)),
        ],
        compiler_params=pltpu.CompilerParams(
            collective_id=0, has_side_effects=True, vmem_limit_bytes=60 * 2**20
        ),
        name="layer",
    )(resid, context, out_weight, gain, order, choices, gate_up, down_weight)


def per_device(
    resid,
    context,
    out_weight,
    norm_gain,
    gate_up,
    down_weight,
    expert_ids,
    slots,
    token_order,
    combine,
):
    tok_rows, half_width = resid.shape
    members, capacity = token_order.shape
    halves = jnp.arange(2, dtype=jnp.int32)[None, :, None] * tok_rows
    order = jnp.where(token_order[:, None, :] >= 0, token_order[:, None, :] + halves, -1)
    live = slots >= 0
    place = jnp.where(live, expert_ids * (2 * capacity) + slots, -1).astype(jnp.float32)
    choices = jnp.concatenate([place, jnp.where(live, combine, 0.0)], axis=1)
    return layer(
        resid,
        context,
        out_weight,
        norm_gain.reshape(1, 2 * half_width),
        order.reshape(members * 2 * capacity, 1),
        choices,
        gate_up,
        down_weight,
    )


def solution(mesh):
    placed = (
        P(("group", "expert"), "tensor"),
        P(("group", "expert"), None),
        P("expert", "tensor"),
        P(),
        P("expert", None, None, "tensor"),
        P("expert", None, "tensor"),
        P(("group", "expert"), None),
        P(("group", "expert"), None),
        P(("group", "expert"), None),
        P(("group", "expert"), None),
    )
    return jax.shard_map(
        per_device,
        mesh=mesh,
        in_specs=placed,
        out_specs=P(("group", "expert"), "tensor"),
        check_vma=False,
    )
```
